256 devices in a mesh: ctx: 32 (over y, z_hi, core), tp: 8 (over x, z_lo).
Axes of the slice: x: 4, y: 4, z: 8 (z_hi: 4, z_lo: 2; z = z_hi * 2 + z_lo), core: 2. Of those that a mesh axis runs over, the one named last changes fastest.
Arguments:
- queries: bfloat16 [1024, 4096], P(None, 'tp'), may hold values from -48 to 48
- prefix_keys: bfloat16 [32768, 4096], P('ctx', 'tp'), may hold values from -30 to 30
- prefix_values: bfloat16 [32768, 4096], P('ctx', 'tp'), may hold values from -24 to 24
- out_weight: bfloat16 [4096, 4096], P('tp'), may hold values from -0.09375 to 0.09375
- out_grad: bfloat16 [1024, 4096], P('ctx', 'tp'), may hold values from -6 to 6
Outputs:
- latent_out: bfloat16 [1024, 4096], P('ctx', 'tp')
- query_grad: bfloat16 [1024, 4096], P('ctx', 'tp')
- key_grad: bfloat16 [32768, 4096], P('ctx', 'tp')
- value_grad: bfloat16 [32768, 4096], P('ctx', 'tp')
- weight_grad: float32 [4096, 4096], P('tp', 'ctx')
The draws below stay inside these ranges and needn't reach their ends.
All inputs are finite; a program needn't handle non-finite values.
Results may differ from the reference program's by a relative error of at most 0.039.
Values may be sent and summed in bfloat16 or wider, within the bound.
No kernel may reach another device: no remote copies, remote signals or barrier semaphores. Data moves between devices by JAX's collectives and lax.ppermute only.
A program may use at most 128 MiB of HBM per device.

```python
import jax
import jax.numpy as jnp
from jax import lax

D = 4096
HEADS = 32
HDIM = 128
LAT = 1024
PREFIX = 32768


def shared_parts(key):
    base_keys = jnp.clip(jax.random.normal(jax.random.fold_in(key, 11), (PREFIX, HEADS * HDIM), jnp.float32), -6.0, 6.0)
    return base_keys


def draw_prefix_keys(key, part):
    base_keys = shared_parts(key)
    return base_keys.astype(jnp.bfloat16)


def draw_queries(key, part):
    key = jax.random.fold_in(key, 5)
    drawn = 2.5 * jnp.clip(jax.random.normal(key, (LAT, HEADS * HDIM), jnp.float32), -6.0, 6.0)
    return drawn.astype(jnp.bfloat16)


def with_spikes(result, key, source, target, blocks, factor):
    owner, partner = [(jnp.arange(result.shape[position]) // (result.shape[position] // blocks)).reshape([-1 if axis == position else 1 for axis in range(result.ndim)]) for position in (source, target)]
    chosen = jax.random.permutation(key, blocks)[partner]
    strong = (owner == chosen) | (owner == (partner + blocks // 2) % blocks)
    return jnp.where(strong, factor * result, result)


def block_levels(key, shape, shards, smallest, top_value):
    def one(dim, blocks):
        heights = jax.random.uniform(jax.random.fold_in(jax.random.fold_in(key, 6), dim), (blocks,), jnp.float32, smallest / len(shards), top_value / len(shards))
        return jnp.repeat(jnp.exp(heights), shape[dim] // blocks).reshape((-1,) + (1,) * (len(shape) - dim - 1))

    loudness = one(*shards[0])
    for cut in shards[1:]:
        loudness = loudness * one(*cut)
    return loudness


def gaussian(stream_key, extent, scale, bound, shards=(), kind=jnp.bfloat16):
    drawn = scale * jax.random.normal(stream_key, extent, jnp.float32)
    if shards:
        drawn = drawn * block_levels(stream_key, extent, shards, -0.22, 0.18)
    return jnp.clip(drawn, -bound, bound).astype(kind)


def heavy_noise(own_key, shape, deviation, bound, shards, heavy, kind=jnp.bfloat16):
    values = deviation * jax.random.normal(own_key, shape, jnp.float32)
    if shards:
        values = values * block_levels(own_key, shape, shards, -0.22, 0.18)
    return jnp.clip(with_spikes(values, jax.random.fold_in(own_key, 3), *heavy), -bound, bound).astype(kind)


def setup_inputs(seed: int = 0) -> dict:
    splits = jax.random.split(jax.random.key(seed), 6)
    return {
        "queries": draw_queries(jax.random.fold_in(splits[5], 71), 0),
        "prefix_keys": draw_prefix_keys(jax.random.fold_in(splits[5], 71), 0),
        "prefix_values": gaussian(splits[2], (PREFIX, HEADS * HDIM), 4.0, 24.0, ((0, 32), (1, 8))),
        "out_weight": gaussian(splits[3], (HEADS * HDIM, D), (HEADS * HDIM) ** -0.5, 0.09375, ((0, 8),)),
        "out_grad": heavy_noise(splits[4], (LAT, D), 1.0, 6.0, ((0, 32), (1, 8)), (0, 1, 32, 2.75)),
    }


def head_forward(operands):
    query_part, key_part, value_part = operands
    scale = HDIM ** -0.5
    scores = jnp.dot(query_part, key_part.T, preferred_element_type=jnp.float32) * scale
    row_top = jnp.max(scores, axis=1, keepdims=True)
    expo = jnp.exp(scores - row_top)
    denom = jnp.sum(expo, axis=1, keepdims=True)
    numer = jnp.dot(expo.astype(jnp.bfloat16), value_part, preferred_element_type=jnp.float32)
    attended = (numer / denom).astype(jnp.bfloat16)
    log_den = row_top + jnp.log(denom)
    return attended, log_den


def head_backward(operands):
    query_part, key_part, value_part, attended, dout, log_den = operands
    scale = HDIM ** -0.5
    scores = jnp.dot(query_part, key_part.T, preferred_element_type=jnp.float32) * scale
    probs = jnp.exp(scores - log_den)
    delta = jnp.sum(dout.astype(jnp.float32) * attended.astype(jnp.float32), axis=1, keepdims=True)
    value_grad = jnp.dot(probs.astype(jnp.bfloat16).T, dout, preferred_element_type=jnp.float32)
    dprob = jnp.dot(dout, value_part.T, preferred_element_type=jnp.float32)
    dscore = (probs * (dprob - delta) * scale).astype(jnp.bfloat16)
    query_grad = jnp.dot(dscore, key_part, preferred_element_type=jnp.float32)
    key_grad = jnp.dot(dscore.T, query_part, preferred_element_type=jnp.float32)
    return query_grad.astype(jnp.bfloat16), key_grad.astype(jnp.bfloat16), value_grad.astype(jnp.bfloat16)


def split_heads(matrix):
    return matrix.reshape(matrix.shape[0], HEADS, HDIM).transpose(1, 0, 2)


def join_heads(stacked):
    return stacked.transpose(1, 0, 2).reshape(stacked.shape[1], HEADS * HDIM)


def reference(queries, prefix_keys, prefix_values, out_weight, out_grad):
    query_heads = split_heads(queries)
    key_heads = split_heads(prefix_keys)
    value_heads = split_heads(prefix_values)
    attended, log_den = lax.map(head_forward, (query_heads, key_heads, value_heads))
    flat = join_heads(attended)
    latent_out = jnp.dot(flat, out_weight, preferred_element_type=jnp.float32).astype(jnp.bfloat16)
    weight_grad = jnp.dot(flat.T, out_grad, preferred_element_type=jnp.float32)
    dout = jnp.dot(out_grad, out_weight.T, preferred_element_type=jnp.float32).astype(jnp.bfloat16)
    dout_heads = split_heads(dout)
    query_grad, key_grad, value_grad = lax.map(head_backward, (query_heads, key_heads, value_heads, attended, dout_heads, log_den))
    return latent_out, join_heads(query_grad), join_heads(key_grad), join_heads(value_grad), weight_grad
```

```python
import functools
import math

import jax
import jax.numpy as jnp
from jax import lax
from jax.experimental import pallas as pl
from jax.experimental.pallas import tpu as pltpu
from jax.sharding import Mesh
from jax.sharding import PartitionSpec as P

HDIM = 128
SCALE = HDIM ** (-0.5)
LOG2E = math.log2(math.e)
EXP2_SCALE = SCALE * LOG2E
CHIPS = ("y", "zh")
CTX = ("y", "zh", "core")
TP = ("x", "zl")
N_CHIPS = 16
HEADS_HERE = 2
WIDE = HEADS_HERE * HDIM
NUM, DOUT, COT, STAT = 64, 64, 32, 16
ROWS1 = NUM + DOUT + COT + STAT
ROWS2 = NUM + STAT
F32 = jnp.float32
BF16 = jnp.bfloat16
VMEM_BYTES = 50 * 1024 * 1024


def dot(a, b, ca, cb):
    return lax.dot_general(a, b, (((ca,), (cb,)), ((), ())), preferred_element_type=F32)


def in_three(x):
    high = x.astype(BF16)
    rest = x - high.astype(F32)
    middle = rest.astype(BF16)
    low = (rest - middle.astype(F32)).astype(BF16)
    return high, middle, low


def of_three(block, at):
    return (
        block[at : at + 1, :].astype(F32)
        + block[at + 1 : at + 2, :].astype(F32)
        + block[at + 2 : at + 3, :].astype(F32)
    )


def forward_kernel(core_ref, q_ref, ko_ref, kr_ref, vo_ref, vr_ref, dout_ref, cot_ref, msg_ref):
    pieces = []
    for h in range(HEADS_HERE):
        cols = slice(h * HDIM, (h + 1) * HDIM)
        q = q_ref[:, cols]
        scores = [dot(k[:, cols], q, 1, 1) for k in (ko_ref, kr_ref)]
        top = jnp.maximum(
            jnp.max(scores[0], axis=0, keepdims=True), jnp.max(scores[1], axis=0, keepdims=True)
        )
        shift = top * EXP2_SCALE
        expo = [jnp.exp2(s * EXP2_SCALE - shift) for s in scores]
        den = jnp.sum(expo[0], axis=0, keepdims=True) + jnp.sum(expo[1], axis=0, keepdims=True)
        num = dot(vo_ref[:, cols], expo[0].astype(BF16), 0, 0) + dot(
            vr_ref[:, cols], expo[1].astype(BF16), 0, 0
        )
        part = jnp.transpose(num / den).astype(BF16)
        msg_ref[:, 0:NUM, cols] = part.reshape(4, NUM, HDIM)
        pieces.extend(in_three(top * SCALE + jnp.log(den)))
    for d in range(4):
        msg_ref[d, NUM : NUM + DOUT, :] = dout_ref[...]
        msg_ref[d, NUM + DOUT : NUM + DOUT + COT, :] = cot_ref[
            d // 2, :, (d % 2) * WIDE : (d % 2 + 1) * WIDE
        ]
    stats = jnp.concatenate(pieces + [jnp.zeros((STAT - 6, WIDE), BF16)], axis=0)
    for d in range(4):
        msg_ref[d, NUM + DOUT + COT :, :] = stats


def forward(core, queries, keys, keys_in, values, values_in, dout64, cot):
    tokens = keys.shape[0]
    grid_spec = pltpu.PrefetchScalarGridSpec(
        num_scalar_prefetch=1,
        grid=(4,),
        in_specs=[
            pl.BlockSpec((WIDE, WIDE), lambda i, c: (i, c[0])),
            pl.BlockSpec((tokens, WIDE), lambda i, c: (0, c[0])),
            pl.BlockSpec((tokens, WIDE), lambda i, c: (0, 0)),
            pl.BlockSpec((tokens, WIDE), lambda i, c: (0, c[0])),
            pl.BlockSpec((tokens, WIDE), lambda i, c: (0, 0)),
            pl.BlockSpec((DOUT, WIDE), lambda i, c: (0, 0)),
            pl.BlockSpec((2, COT, 2 * WIDE), lambda i, c: (i, 0, 0)),
        ],
        out_specs=pl.BlockSpec((4, ROWS1, WIDE), lambda i, c: (i, 0, 0)),
    )
    return pl.pallas_call(
        forward_kernel,
        out_shape=jax.ShapeDtypeStruct((N_CHIPS, ROWS1, WIDE), BF16),
        grid_spec=grid_spec,
        compiler_params=pltpu.CompilerParams(vmem_limit_bytes=VMEM_BYTES),
        name="forward",
    )(core, queries, keys, keys_in, values, values_in, dout64, cot)


def combine_kernel(zh_ref, num_ref, stat_ref, dout_ref, msg_ref):
    zh = zh_ref[0]
    lanes = lax.broadcasted_iota(jnp.int32, (1, WIDE), 1)
    pieces = []
    deltas = []
    att_all = []
    for h in range(HEADS_HERE):
        cols = slice(h * HDIM, (h + 1) * HDIM)
        lse = jnp.concatenate([of_three(stat_ref[c], 3 * h) for c in range(N_CHIPS)], axis=0)
        mine = jnp.zeros((N_CHIPS, NUM), F32)
        for z in range(4):
            mine = jnp.where(zh == z, lse[:, z * NUM : (z + 1) * NUM], mine)
        top = jnp.max(mine, axis=0, keepdims=True)
        total = top + jnp.log(jnp.sum(jnp.exp(mine - top), axis=0, keepdims=True))
        weight = jnp.transpose(jnp.exp(mine - total))
        att = jnp.zeros((NUM, HDIM), F32)
        for c in range(N_CHIPS):
            att = att + num_ref[c, :, cols].astype(F32) * weight[:, c : c + 1]
        att = att.astype(BF16)
        att_all.append(att)
        delta = jnp.sum(att.astype(F32) * dout_ref[:, cols].astype(F32), axis=1, keepdims=True)
        pieces.extend(in_three(total))
        deltas.extend(in_three(jnp.transpose(jnp.broadcast_to(delta, (NUM, HDIM)))[0:1, :]))
    stats = jnp.concatenate(pieces + deltas + [jnp.zeros((STAT - 12, NUM), BF16)], axis=0)
    stats = jnp.concatenate([stats, jnp.zeros((STAT, WIDE - NUM), BF16)], axis=1)
    att = jnp.concatenate(att_all, axis=1)
    for c in range(N_CHIPS):
        msg_ref[c, 0:NUM, :] = att
        msg_ref[c, NUM:, :] = stats


def combine(zh, msg, dout64):
    grid_spec = pltpu.PrefetchScalarGridSpec(
        num_scalar_prefetch=1,
        grid=(1,),
        in_specs=[
            pl.BlockSpec((N_CHIPS, NUM, WIDE), lambda i, z: (0, 0, 0)),
            pl.BlockSpec((N_CHIPS, STAT, WIDE), lambda i, z: (0, (ROWS1 - STAT) // STAT, 0)),
            pl.BlockSpec((DOUT, WIDE), lambda i, z: (0, 0)),
        ],
        out_specs=pl.BlockSpec((N_CHIPS, ROWS2, WIDE), lambda i, z: (0, 0, 0)),
    )
    return pl.pallas_call(
        combine_kernel,
        out_shape=jax.ShapeDtypeStruct((N_CHIPS, ROWS2, WIDE), BF16),
        grid_spec=grid_spec,
        compiler_params=pltpu.CompilerParams(vmem_limit_bytes=VMEM_BYTES),
        name="combine",
    )(zh, msg, msg, dout64)


def backward_kernel(
    core_ref, q_ref, dout_ref, stat_ref, ko_ref, kr_ref, vo_ref, vr_ref,
    dq_ref, dko_ref, dkr_ref, dvo_ref, dvr_ref, dq_acc, stat_acc,
):
    step = pl.program_id(0)
    latents = q_ref.shape[0]

    @pl.when(step == 0)
    def _():
        dq_acc[...] = jnp.zeros_like(dq_acc)
        for pair in range(N_CHIPS // 2):
            both = []
            for c in (2 * pair, 2 * pair + 1):
                block = stat_ref[c]
                both.append(
                    jnp.concatenate([of_three(block, 3 * r)[:, :NUM] for r in range(4)], axis=0)
                )
            stat_acc[0:4, pair * 2 * NUM : (pair + 1) * 2 * NUM] = jnp.concatenate(both, axis=1)

    for h in range(HEADS_HERE):
        cols = slice(h * HDIM, (h + 1) * HDIM)
        q = q_ref[:, cols]
        dout = dout_ref[:, :, cols].reshape(latents, HDIM)
        lse = stat_acc[h : h + 1, :] * LOG2E
        delta = stat_acc[2 + h : 3 + h, :]
        for k_ref, v_ref, dk_ref, dv_ref in (
            (ko_ref, vo_ref, dko_ref, dvo_ref),
            (kr_ref, vr_ref, dkr_ref, dvr_ref),
        ):
            k = k_ref[:, cols]
            scores = dot(k, q, 1, 1)
            probs = jnp.exp2(scores * EXP2_SCALE - lse)
            dprob = dot(v_ref[:, cols], dout, 1, 1)
            dscore = (probs * (dprob - delta)).astype(BF16)
            dv_ref[:, cols] = dot(probs.astype(BF16), dout, 1, 0).astype(BF16)
            dk_ref[:, cols] = (dot(dscore, q, 1, 0) * SCALE).astype(BF16)
            dq_acc[cols, :] += dot(k, dscore, 0, 0)

    @pl.when(step == pl.num_programs(0) - 1)
    def _():
        dq_ref[...] = jnp.transpose(dq_acc[...] * SCALE).astype(BF16)


def backward(core, queries, msg1, msg2, keys, keys_in, values, values_in):
    latents = queries.shape[0]
    tokens = keys.shape[0]
    block = 256
    own = pl.BlockSpec((block, WIDE), lambda i, c: (i, c[0]))
    plain = pl.BlockSpec((block, WIDE), lambda i, c: (i, 0))
    grid_spec = pltpu.PrefetchScalarGridSpec(
        num_scalar_prefetch=1,
        grid=(tokens // block,),
        in_specs=[
            pl.BlockSpec((latents, WIDE), lambda i, c: (0, c[0])),
            pl.BlockSpec((N_CHIPS, DOUT, WIDE), lambda i, c: (0, 1, 0)),
            pl.BlockSpec((N_CHIPS, STAT, WIDE), lambda i, c: (0, NUM // STAT, 0)),
            own, plain, own, plain,
        ],
        out_specs=[
            pl.BlockSpec((latents, WIDE), lambda i, c: (0, 0)),
            plain, plain, plain, plain,
        ],
        scratch_shapes=[pltpu.VMEM((WIDE, latents), F32), pltpu.VMEM((8, latents), F32)],
    )
    part = jax.ShapeDtypeStruct((tokens, WIDE), BF16)
    return pl.pallas_call(
        backward_kernel,
        out_shape=[jax.ShapeDtypeStruct((latents, WIDE), BF16), part, part, part, part],
        grid_spec=grid_spec,
        compiler_params=pltpu.CompilerParams(vmem_limit_bytes=VMEM_BYTES),
        name="backward",
    )(core, queries, msg1, msg2, keys, keys_in, values, values_in)


def swap(x):
    return lax.ppermute(x, "core", [(0, 1), (1, 0)])


def half(x, index, axis):
    size = x.shape[axis] // 2
    return lax.dynamic_slice_in_dim(x, index * size, size, axis)


def in_order(core, mine, other, axis):
    return jnp.where(
        core == 0,
        jnp.concatenate([mine, other], axis),
        jnp.concatenate([other, mine], axis),
    )


def gather(x, axes, size):
    tiled = jnp.broadcast_to(x[None], (size,) + x.shape)
    return lax.all_to_all(tiled, axes, 0, 0, tiled=True)


def body(queries, prefix_keys, prefix_values, out_weight, out_grad):
    core = lax.axis_index("core")
    core_arr = core.astype(jnp.int32).reshape(1)
    zh_arr = lax.axis_index("zh").astype(jnp.int32).reshape(1)
    keys_in = swap(half(prefix_keys, 1 - core, 1))
    values_in = swap(half(prefix_values, 1 - core, 1))

    cot = gather(out_grad, TP, 8)
    cot_rows = jnp.concatenate([cot[i] for i in range(8)], axis=1)
    dout32 = dot(cot_rows, out_weight, 1, 1).astype(BF16)
    dout_in = swap(half(dout32, 1 - core, 1))
    dout64 = in_order(core, half(dout32, core, 1), dout_in, 0)

    msg1 = forward(
        core_arr, queries, prefix_keys, keys_in, prefix_values, values_in, dout64, cot
    )
    msg1 = lax.all_to_all(msg1, CHIPS, 0, 0, tiled=True)
    msg2 = combine(zh_arr, msg1, dout64)
    att64 = msg2[0, :NUM]
    att32 = in_order(core, half(att64, core, 0), swap(half(att64, 1 - core, 0)), 1)
    partial_out = dot(att32, out_weight, 1, 0).astype(BF16)
    latent_out = lax.psum_scatter(partial_out, TP, scatter_dimension=1, tiled=True)

    msg2 = lax.all_to_all(msg2, CHIPS, 0, 0, tiled=True)
    dq, dko, dkr, dvo, dvr = backward(
        core_arr, queries, msg1, msg2, prefix_keys, keys_in, prefix_values, values_in
    )
    dk_in = swap(dkr)
    dv_in = swap(dvr)

    cot_mine = msg1[:, NUM + DOUT : NUM + DOUT + COT, :]
    cot_all = in_order(core, cot_mine, swap(cot_mine), 1).reshape(N_CHIPS * NUM, WIDE)
    att_all = msg2[:, :NUM, :].reshape(N_CHIPS * NUM, WIDE)
    weight_part = dot(att_all, cot_all, 0, 0)
    weight_grad = in_order(
        core, half(weight_part, core, 1), swap(half(weight_part, 1 - core, 1)), 0
    )

    dq = lax.all_to_all(dq.reshape(N_CHIPS, NUM, WIDE), CHIPS, 0, 0, tiled=True)
    dq64 = jnp.sum(dq.astype(F32), axis=0).astype(BF16)
    query_grad = in_order(core, half(dq64, core, 0), swap(half(dq64, 1 - core, 0)), 1)
    key_grad = in_order(core, dko, dk_in, 1)
    value_grad = in_order(core, dvo, dv_in, 1)
    return latent_out, query_grad, key_grad, value_grad, weight_grad


def solution(mesh):
    fine = Mesh(mesh.devices.reshape(4, 4, 2, 4, 2), ("y", "zh", "core", "x", "zl"))
    placed = (P(None, TP), P(CTX, TP), P(CTX, TP), P(TP, None), P(CTX, TP))
    return jax.shard_map(
        body,
        mesh=fine,
        in_specs=placed,
        out_specs=(P(CTX, TP), P(CTX, TP), P(CTX, TP), P(CTX, TP), P(TP, CTX)),
        check_vma=False,
    )
```

```python
import math

import jax
import jax.numpy as jnp
from jax import lax
from jax.experimental import pallas as pl
from jax.experimental.pallas import tpu as pltpu
from jax.sharding import Mesh
from jax.sharding import PartitionSpec as P

HDIM = 128
SCALE = HDIM ** (-0.5)
LOG2E = math.log2(math.e)
EXP2_SCALE = SCALE * LOG2E
CHIPS = ("y", "zh")
CTX = ("y", "zh", "core")
TP = ("x", "zl")
N_CHIPS = 16
HEADS_HERE = 2
WIDE = HEADS_HERE * HDIM
NUM, STAT, COT = 64, 48, 32
ROWS1 = NUM + STAT
ROWS2 = NUM + NUM + COT
LATENTS = N_CHIPS * NUM
F32 = jnp.float32
BF16 = jnp.bfloat16


def dot(a, b, ca, cb):
    return lax.dot_general(a, b, (((ca,), (cb,)), ((), ())), preferred_element_type=F32)


def in_three(x):
    high = x.astype(BF16)
    rest = x - high.astype(F32)
    middle = rest.astype(BF16)
    low = (rest - middle.astype(F32)).astype(BF16)
    return high, middle, low


def params(mib):
    return pltpu.CompilerParams(vmem_limit_bytes=mib * 1024 * 1024)


def whole(*shape):
    return pl.BlockSpec(shape, lambda *_: (0,) * len(shape))


def head_cols(h):
    return slice(h * HDIM, (h + 1) * HDIM)


def dout_kernel(place_ref, own_ref, other_ref, w_ref, out_ref, cot_ref):
    core = place_ref[0]
    for row, ref in ((core, own_ref), (1 - core, other_ref)):
        start = pl.multiple_of(row * COT, COT)
        for b in range(8):
            cot_ref[pl.ds(start, COT), b * 512 : (b + 1) * 512] = ref[b]
    dout = jnp.transpose(dot(w_ref[...], cot_ref[...], 1, 1)).astype(BF16)
    for c in range(N_CHIPS):
        out_ref[c] = dout


def dout_rows(place, cot, cot_in, out_weight):
    depth = out_weight.shape[1]
    grid_spec = pltpu.PrefetchScalarGridSpec(
        num_scalar_prefetch=1,
        grid=(1,),
        in_specs=[
            whole(8, COT, 512),
            whole(8, COT, 512),
            pl.BlockSpec((WIDE, depth), lambda i, c: (c[0], 0)),
        ],
        out_specs=whole(N_CHIPS, NUM, WIDE),
        scratch_shapes=[pltpu.VMEM((NUM, depth), BF16)],
    )
    return pl.pallas_call(
        dout_kernel,
        out_shape=jax.ShapeDtypeStruct((N_CHIPS, NUM, WIDE), BF16),
        grid_spec=grid_spec,
        compiler_params=params(60),
        name="dout",
    )(place, cot, cot_in, out_weight)


def forward_kernel(place_ref, q_ref, ko_ref, kr_ref, vo_ref, vr_ref, part_ref, lse_ref):
    heads = range(HEADS_HERE)
    scores = [
        [dot(k[:, head_cols(h)], q_ref[:, head_cols(h)], 1, 1) for k in (ko_ref, kr_ref)]
        for h in heads
    ]
    expos = []
    for h in heads:
        top = jnp.maximum(
            jnp.max(scores[h][0], axis=0, keepdims=True),
            jnp.max(scores[h][1], axis=0, keepdims=True),
        )
        shift = top * EXP2_SCALE
        expo = [jnp.exp2(s * EXP2_SCALE - shift) for s in scores[h]]
        den = jnp.sum(expo[0], axis=0, keepdims=True) + jnp.sum(expo[1], axis=0, keepdims=True)
        expos.append(([e.astype(BF16) for e in expo], den))
        lse_ref[h : h + 1, :] = top * SCALE + jnp.log(den)
    for h in heads:
        (own, other), den = expos[h]
        num = dot(vo_ref[:, head_cols(h)], own, 0, 0) + dot(vr_ref[:, head_cols(h)], other, 0, 0)
        part_ref[:, head_cols(h)] = jnp.transpose(num / den).astype(BF16)


def forward(place, queries, keys, keys_in, values, values_in):
    tokens = keys.shape[0]
    block = 512
    own = pl.BlockSpec((tokens, WIDE), lambda i, c: (0, c[0]))
    grid_spec = pltpu.PrefetchScalarGridSpec(
        num_scalar_prefetch=1,
        grid=(LATENTS // block,),
        in_specs=[
            pl.BlockSpec((block, WIDE), lambda i, c: (i, c[0])),
            own, own, own, own,
        ],
        out_specs=[
            pl.BlockSpec((block, WIDE), lambda i, c: (i, 0)),
            pl.BlockSpec((8, block), lambda i, c: (0, i)),
        ],
    )
    return pl.pallas_call(
        forward_kernel,
        out_shape=[
            jax.ShapeDtypeStruct((LATENTS, WIDE), BF16),
            jax.ShapeDtypeStruct((8, LATENTS), F32),
        ],
        grid_spec=grid_spec,
        compiler_params=params(60),
        cost_estimate=pl.CostEstimate(
            flops=9_000_000_000, bytes_accessed=4_000_000, transcendentals=4_194_304
        ),
        name="forward",
    )(place, queries, keys, keys_in, values, values_in)


def message_kernel(part_ref, lse_ref, dout_ref, msg_ref, stat_ref):
    rows = []
    deltas = []
    stat_ref[...] = jnp.zeros_like(stat_ref)
    for h in range(HEADS_HERE):
        cols = head_cols(h)
        dout = dout_ref[:, :, cols].reshape(LATENTS, HDIM).astype(F32)
        delta = jnp.sum(part_ref[:, cols].astype(F32) * dout, axis=1, keepdims=True)
        deltas.append(jnp.transpose(jnp.broadcast_to(delta, (LATENTS, HDIM)))[0:1, :])
        stat_ref[h : h + 1, :] = lse_ref[h : h + 1, :] * LOG2E
        stat_ref[2 + h : 3 + h, :] = deltas[h]
    for h in range(HEADS_HERE):
        rows.extend(in_three(lse_ref[h : h + 1, :]))
    for h in range(HEADS_HERE):
        rows.extend(in_three(deltas[h]))
    stats = jnp.concatenate(rows, axis=0)
    stats = jnp.concatenate([stats[:, i * WIDE : (i + 1) * WIDE] for i in range(4)], axis=0)
    for c in range(N_CHIPS):
        msg_ref[c, 0:NUM, :] = part_ref[c * NUM : (c + 1) * NUM, :]
        msg_ref[c, NUM:, :] = stats


def message(part, lse, dout):
    return pl.pallas_call(
        message_kernel,
        out_shape=[
            jax.ShapeDtypeStruct((N_CHIPS, ROWS1, WIDE), BF16),
            jax.ShapeDtypeStruct((8, LATENTS), F32),
        ],
        grid=(1,),
        in_specs=[whole(LATENTS, WIDE), whole(8, LATENTS), whole(N_CHIPS, NUM, WIDE)],
        out_specs=[whole(N_CHIPS, ROWS1, WIDE), whole(8, LATENTS)],
        compiler_params=params(60),
        name="message",
    )(part, lse, dout)


def combine_kernel(
    place_ref, msg_ref, cot_ref, own_ref, a_ref, b_ref, att_ref, stat_ref, out_ref
):
    y = place_ref[1]
    zh = place_ref[2]
    mine = [jnp.zeros((N_CHIPS, WIDE), F32) for _ in range(HEADS_HERE)]
    stat_ref[...] = jnp.zeros_like(stat_ref)
    for i in range(4):
        blocks = [msg_ref[c, NUM:, :].astype(F32) for c in range(N_CHIPS)]
        cols = slice(i * WIDE, (i + 1) * WIDE)

        def value(r):
            at = 12 * i + 3 * r
            return jnp.concatenate(
                [b[at : at + 1] + b[at + 1 : at + 2] + b[at + 2 : at + 3] for b in blocks], axis=0
            )

        for h in range(HEADS_HERE):
            lse = value(h)
            delta = value(2 + h)
            top = jnp.max(lse, axis=0, keepdims=True)
            total = top + jnp.log(jnp.sum(jnp.exp(lse - top), axis=0, keepdims=True))
            weight = jnp.exp(lse - total)
            stat_ref[h : h + 1, cols] = total * LOG2E
            stat_ref[2 + h : 3 + h, cols] = jnp.sum(weight * delta, axis=0, keepdims=True)
            mine[h] = jnp.where(y == i, weight, mine[h])
    att_all = []
    for h in range(HEADS_HERE):
        rows = jnp.zeros((N_CHIPS, NUM), F32)
        for z in range(4):
            rows = jnp.where(zh == z, mine[h][:, z * NUM : (z + 1) * NUM], rows)
        weight = jnp.transpose(rows)
        att = jnp.zeros((NUM, HDIM), F32)
        for c in range(N_CHIPS):
            att = att + msg_ref[c, 0:NUM, head_cols(h)].astype(F32) * weight[:, c : c + 1]
        att_all.append(att.astype(BF16))
    att = jnp.concatenate(att_all, axis=1)
    att_ref[...] = att
    for c in range(N_CHIPS):
        out_ref[c, NUM : 2 * NUM, :] = att
        out_ref[c, 2 * NUM :, :] = cot_ref[c // 2, :, c % 2 * WIDE : (c % 2 + 1) * WIDE]
    for h in range(HEADS_HERE):
        cols = head_cols(h)
        share = jnp.exp2(own_ref[h : h + 1, :] - stat_ref[h : h + 1, :]) * SCALE
        rest = stat_ref[2 + h : 3 + h, :] - own_ref[2 + h : 3 + h, :]
        dq = jnp.transpose(share * (a_ref[cols, :] - rest * b_ref[cols, :])).astype(BF16)
        out_ref[:, 0:NUM, cols] = dq.reshape(N_CHIPS, NUM, HDIM)


def combine(place, msg, cot, own_stats, a, b):
    grid_spec = pltpu.PrefetchScalarGridSpec(
        num_scalar_prefetch=1,
        grid=(1,),
        in_specs=[
            whole(N_CHIPS, ROWS1, WIDE), whole(8, COT, 512), whole(8, LATENTS),
            whole(WIDE, LATENTS), whole(WIDE, LATENTS),
        ],
        out_specs=[whole(NUM, WIDE), whole(8, LATENTS), whole(N_CHIPS, ROWS2, WIDE)],
    )
    return pl.pallas_call(
        combine_kernel,
        out_shape=[
            jax.ShapeDtypeStruct((NUM, WIDE), BF16),
            jax.ShapeDtypeStruct((8, LATENTS), F32),
            jax.ShapeDtypeStruct((N_CHIPS, ROWS2, WIDE), BF16),
        ],
        grid_spec=grid_spec,
        compiler_params=params(24),
        name="combine",
    )(place, msg, cot, own_stats, a, b)


def query_kernel(
    place_ref, q_ref, dout_ref, stat_ref, ko_ref, kr_ref, vo_ref, vr_ref,
    a_ref, b_ref, prob_ref, score_ref,
):
    h = pl.program_id(0)
    block = 256
    for src, (k_ref, v_ref) in enumerate(((ko_ref, vo_ref), (kr_ref, vr_ref))):
        k = k_ref[...]
        v = v_ref[...]
        for at in range(0, LATENTS, block):
            rows = slice(at, at + block)
            q = q_ref[rows, :]
            dout = dout_ref[at // NUM : (at + block) // NUM].reshape(block, HDIM)
            lse = stat_ref[pl.ds(h, 1), rows]
            delta = stat_ref[pl.ds(2 + h, 1), rows]
            probs = jnp.exp2(dot(k, q, 1, 1) * EXP2_SCALE - lse)
            dscore = (probs * (dot(v, dout, 1, 1) - delta)).astype(BF16)
            probs = probs.astype(BF16)
            prob_ref[0, src, :, rows] = probs
            score_ref[0, src, :, rows] = dscore
            a = dot(k, dscore, 0, 0)
            b = dot(k, probs, 0, 0)
            if src == 0:
                a_ref[:, rows] = a
                b_ref[:, rows] = b
            else:
                a_ref[:, rows] += a
                b_ref[:, rows] += b


def query_parts(place, queries, dout, stats, keys, keys_in, values, values_in):
    tokens = keys.shape[0]
    head = pl.BlockSpec((tokens, HDIM), lambda h, c: (0, c[0] * HEADS_HERE + h))
    sums = pl.BlockSpec((HDIM, LATENTS), lambda h, c: (h, 0))
    kept = pl.BlockSpec((1, 2, tokens, LATENTS), lambda h, c: (h, 0, 0, 0))
    grid_spec = pltpu.PrefetchScalarGridSpec(
        num_scalar_prefetch=1,
        grid=(HEADS_HERE,),
        in_specs=[
            pl.BlockSpec((LATENTS, HDIM), lambda h, c: (0, c[0] * HEADS_HERE + h)),
            pl.BlockSpec((N_CHIPS, NUM, HDIM), lambda h, c: (0, 0, h)),
            whole(8, LATENTS),
            head, head, head, head,
        ],
        out_specs=[sums, sums, kept, kept],
    )
    return pl.pallas_call(
        query_kernel,
        out_shape=[
            jax.ShapeDtypeStruct((WIDE, LATENTS), F32),
            jax.ShapeDtypeStruct((WIDE, LATENTS), F32),
            jax.ShapeDtypeStruct((HEADS_HERE, 2, tokens, LATENTS), BF16),
            jax.ShapeDtypeStruct((HEADS_HERE, 2, tokens, LATENTS), BF16),
        ],
        grid_spec=grid_spec,
        compiler_params=params(60),
        cost_estimate=pl.CostEstimate(
            flops=12_000_000_000, bytes_accessed=20_000_000, transcendentals=4_194_304
        ),
        name="query",
    )(place, queries, dout, stats, keys, keys_in, values, values_in)


def token_kernel(
    place_ref, q_ref, dout_ref, own_ref, stat_ref, prob_ref, score_ref,
    dko_ref, dkr_ref, dvo_ref, dvr_ref, both_ref, q_scaled_ref,
):
    h = pl.program_id(0)

    @pl.when(pl.program_id(1) == 0)
    def _():
        share = jnp.exp2(own_ref[pl.ds(h, 1), :] - stat_ref[pl.ds(h, 1), :])
        rest = share * (own_ref[pl.ds(2 + h, 1), :] - stat_ref[pl.ds(2 + h, 1), :])
        share = jnp.transpose(jnp.broadcast_to(share, (HDIM, LATENTS)))
        rest = jnp.transpose(jnp.broadcast_to(rest, (HDIM, LATENTS)))
        q = q_ref[...].astype(F32)
        dout = dout_ref[...].reshape(LATENTS, HDIM).astype(F32)
        both_ref[:, :HDIM] = (share * dout).astype(BF16)
        both_ref[:, HDIM:] = (rest * q).astype(BF16)
        q_scaled_ref[...] = (share * q).astype(BF16)

    block = dko_ref.shape[0]
    both = dot(prob_ref[0].reshape(2 * block, LATENTS), both_ref[...], 1, 0)
    dk = dot(score_ref[0].reshape(2 * block, LATENTS), q_scaled_ref[...], 1, 0)
    dk = ((dk + both[:, HDIM:]) * SCALE).astype(BF16)
    dv = both[:, :HDIM].astype(BF16)
    dko_ref[...] = dk[:block]
    dkr_ref[...] = dk[block:]
    dvo_ref[...] = dv[:block]
    dvr_ref[...] = dv[block:]


def token_grads(place, queries, dout, own_stats, stats, probs, dscores):
    tokens = probs.shape[2]
    block = 512
    own = pl.BlockSpec((block, HDIM), lambda h, i, c: (i, c[0] * HEADS_HERE + h))
    other = pl.BlockSpec((block, HDIM), lambda h, i, c: (i, h))
    kept = pl.BlockSpec((1, 2, block, LATENTS), lambda h, i, c: (h, 0, i, 0))
    grid_spec = pltpu.PrefetchScalarGridSpec(
        num_scalar_prefetch=1,
        grid=(HEADS_HERE, tokens // block),
        in_specs=[
            pl.BlockSpec((LATENTS, HDIM), lambda h, i, c: (0, c[0] * HEADS_HERE + h)),
            pl.BlockSpec((N_CHIPS, NUM, HDIM), lambda h, i, c: (0, 0, h)),
            whole(8, LATENTS),
            whole(8, LATENTS),
            kept, kept,
        ],
        out_specs=[own, other, own, other],
        scratch_shapes=[pltpu.VMEM((LATENTS, WIDE), BF16), pltpu.VMEM((LATENTS, HDIM), BF16)],
    )
    full = jax.ShapeDtypeStruct((tokens, 2 * WIDE), BF16)
    half_wide = jax.ShapeDtypeStruct((tokens, WIDE), BF16)
    return pl.pallas_call(
        token_kernel,
        out_shape=[full, half_wide, full, half_wide],
        grid_spec=grid_spec,
        compiler_params=params(60),
        cost_estimate=pl.CostEstimate(
            flops=6_000_000_000, bytes_accessed=22_000_000, transcendentals=0
        ),
        name="token",
    )(place, queries, dout, own_stats, stats, probs, dscores)


def weight_kernel(place_ref, att_ref, own_ref, other_ref, out_ref, cot_ref):
    core = place_ref[0]
    cot_ref[:, pl.ds(pl.multiple_of(core * COT, COT), COT), :] = own_ref[...]
    cot_ref[:, pl.ds(pl.multiple_of((1 - core) * COT, COT), COT), :] = other_ref[...]
    att = att_ref[...].reshape(LATENTS, WIDE)
    cot = cot_ref[...].reshape(LATENTS, WIDE)
    out_ref[...] = dot(att, cot, 0, 0)


def weight(place, msg, cot_in):
    grid_spec = pltpu.PrefetchScalarGridSpec(
        num_scalar_prefetch=1,
        grid=(1,),
        in_specs=[
            pl.BlockSpec((N_CHIPS, NUM, WIDE), lambda i, c: (0, 1, 0)),
            pl.BlockSpec((N_CHIPS, COT, WIDE), lambda i, c: (0, 2 * NUM // COT, 0)),
            whole(N_CHIPS, COT, WIDE),
        ],
        out_specs=whole(WIDE, WIDE),
        scratch_shapes=[pltpu.VMEM((N_CHIPS, NUM, WIDE), BF16)],
    )
    return pl.pallas_call(
        weight_kernel,
        out_shape=jax.ShapeDtypeStruct((WIDE, WIDE), F32),
        grid_spec=grid_spec,
        compiler_params=params(24),
        name="weight",
    )(place, msg, msg, cot_in)


def swap(x):
    return lax.ppermute(x, "core", [(0, 1), (1, 0)])


def half(x, index, axis):
    size = x.shape[axis] // 2
    return lax.dynamic_slice_in_dim(x, index * size, size, axis)


def in_order(core, mine, other, axis):
    return jnp.where(
        core == 0,
        jnp.concatenate([mine, other], axis),
        jnp.concatenate([other, mine], axis),
    )


def gather(x, axes, size):
    tiled = jnp.broadcast_to(x[None], (size,) + x.shape)
    return lax.all_to_all(tiled, axes, 0, 0, tiled=True)


def shift(x, axis, d):
    return lax.ppermute(x, axis, [(i, (i + d) % 4) for i in range(4)])


def after(x, *others):
    return lax.optimization_barrier((x,) + others)[0]


def body(queries, prefix_keys, prefix_values, out_weight, out_grad):
    core = lax.axis_index("core")
    at_x, at_zl = lax.axis_index("x"), lax.axis_index("zl")
    place = jnp.stack([core, lax.axis_index("y"), lax.axis_index("zh")]).astype(jnp.int32)
    cot = gather(out_grad, TP, 8)
    keys_in = swap(prefix_keys)
    values_in = swap(prefix_values)
    cot, keys_in, values_in = lax.optimization_barrier((cot, keys_in, values_in))
    tokens = (prefix_keys, keys_in, prefix_values, values_in)

    dout = dout_rows(place, cot, swap(cot), out_weight)
    dout = lax.all_to_all(dout, CHIPS, 0, 0, tiled=True)
    part, lse = forward(place, queries, *tokens)
    msg1, own_stats = message(part, lse, dout)
    msg1 = lax.all_to_all(msg1, CHIPS, 0, 0, tiled=True)
    a, b, probs, dscores = query_parts(place, queries, dout, own_stats, *tokens)

    att64, stats, msg2 = combine(place, msg1, cot, own_stats, a, b)
    msg2 = lax.all_to_all(msg2, CHIPS, 0, 0, tiled=True)

    att32 = in_order(core, half(att64, core, 0), swap(half(att64, 1 - core, 0)), 1)
    partial_out = dot(att32, out_weight, 1, 0).reshape(32, 4, 1024).transpose(1, 0, 2)
    by_x = [
        lax.dynamic_index_in_dim(partial_out, lax.rem(at_x + d, 4), 0, keepdims=False)
        for d in range(4)
    ]
    from_x = [shift(by_x[d].astype(BF16), "x", d) for d in (1, 2, 3)]
    dk, dk_out, dv, dv_out = token_grads(
        place, queries, dout, own_stats, after(stats, by_x[0]), probs, dscores
    )
    own_x, *from_x = lax.optimization_barrier((by_x[0], *from_x, dk))[:4]
    over_x = own_x + sum(x.astype(F32) for x in from_x)
    by_zl = over_x.reshape(32, 2, 512).transpose(1, 0, 2)
    from_zl = lax.ppermute(
        lax.dynamic_index_in_dim(by_zl, 1 - at_zl, 0, keepdims=False).astype(BF16),
        "zl",
        [(0, 1), (1, 0)],
    )
    own_zl = lax.dynamic_index_in_dim(by_zl, at_zl, 0, keepdims=False)
    other_cols = (jnp.int32(0), ((1 - core) * WIDE).astype(jnp.int32))
    key_grad = lax.dynamic_update_slice(dk, swap(dk_out), other_cols)
    value_grad = lax.dynamic_update_slice(dv, swap(dv_out), other_cols)
    from_zl = after(from_zl, key_grad, value_grad)
    latent_out = (own_zl + from_zl.astype(F32)).astype(BF16)

    msg2 = after(msg2, latent_out)
    cot_in = swap(msg2[:, 2 * NUM :])
    dq64 = jnp.sum(msg2[:, :NUM].astype(F32), axis=0).astype(BF16)
    dq_in = swap(half(dq64, 1 - core, 0))
    query_grad = in_order(core, half(dq64, core, 0), dq_in, 1)
    weight_part = weight(place, msg2, cot_in)
    weight_in = swap(half(weight_part, 1 - core, 1))
    weight_grad = in_order(core, half(weight_part, core, 1), weight_in, 0)
    return latent_out, query_grad, key_grad, value_grad, weight_grad


def solution(mesh):
    fine = Mesh(mesh.devices.reshape(4, 4, 2, 4, 2), ("y", "zh", "core", "x", "zl"))
    placed = (P(None, TP), P(CTX, TP), P(CTX, TP), P(TP, None), P(CTX, TP))
    return jax.shard_map(
        body,
        mesh=fine,
        in_specs=placed,
        out_specs=(P(CTX, TP), P(CTX, TP), P(CTX, TP), P(CTX, TP), P(TP, CTX)),
        check_vma=False,
    )
```

```python
import math

import jax
import jax.numpy as jnp
from jax import lax
from jax.experimental import pallas as pl
from jax.experimental.pallas import tpu as pltpu
from jax.sharding import Mesh
from jax.sharding import PartitionSpec as P

HDIM = 128
SCALE = HDIM ** (-0.5)
LOG2E = math.log2(math.e)
EXP2_SCALE = SCALE * LOG2E
CHIPS = ("y", "zh")
CTX = ("y", "zh", "core")
TP = ("x", "zl")
N_CHIPS = 16
HEADS_HERE = 2
WIDE = HEADS_HERE * HDIM
NUM, STAT, COT, PART = 64, 48, 32, 16
ROWS1 = NUM + STAT
ROWS2 = NUM + NUM
ROWS0 = NUM + PART
LATENTS = N_CHIPS * NUM
F32 = jnp.float32
BF16 = jnp.bfloat16


def dot(a, b, ca, cb):
    return lax.dot_general(a, b, (((ca,), (cb,)), ((), ())), preferred_element_type=F32)


def in_three(x):
    high = x.astype(BF16)
    rest = x - high.astype(F32)
    middle = rest.astype(BF16)
    low = (rest - middle.astype(F32)).astype(BF16)
    return high, middle, low


def params(mib):
    return pltpu.CompilerParams(vmem_limit_bytes=mib * 1024 * 1024)


def whole(*shape):
    return pl.BlockSpec(shape, lambda *_: (0,) * len(shape))


def head_cols(h):
    return slice(h * HDIM, (h + 1) * HDIM)


def dout_kernel(place_ref, own_ref, other_ref, w_ref, out_ref, cot_ref):
    core = place_ref[0]
    for row, ref in ((core, own_ref), (1 - core, other_ref)):
        start = pl.multiple_of(row * COT, COT)
        for b in range(8):
            cot_ref[pl.ds(start, COT), b * 512 : (b + 1) * 512] = ref[b]
    dout = jnp.transpose(dot(w_ref[...], cot_ref[...], 1, 1)).astype(BF16)
    start = pl.multiple_of(core * COT + place_ref[3] * PART, PART)
    for c in range(N_CHIPS):
        out_ref[c, 0:NUM, :] = dout
        out_ref[c, NUM:, :] = cot_ref[pl.ds(start, PART), c * WIDE : (c + 1) * WIDE]


def dout_rows(place, cot, cot_in, out_weight):
    depth = out_weight.shape[1]
    grid_spec = pltpu.PrefetchScalarGridSpec(
        num_scalar_prefetch=1,
        grid=(1,),
        in_specs=[
            whole(8, COT, 512),
            whole(8, COT, 512),
            pl.BlockSpec((WIDE, depth), lambda i, c: (c[0], 0)),
        ],
        out_specs=whole(N_CHIPS, ROWS0, WIDE),
        scratch_shapes=[pltpu.VMEM((NUM, depth), BF16)],
    )
    return pl.pallas_call(
        dout_kernel,
        out_shape=jax.ShapeDtypeStruct((N_CHIPS, ROWS0, WIDE), BF16),
        grid_spec=grid_spec,
        compiler_params=params(60),
        name="dout",
    )(place, cot, cot_in, out_weight)


def forward_kernel(place_ref, q_ref, ko_ref, kr_ref, vo_ref, vr_ref, part_ref, lse_ref):
    heads = range(HEADS_HERE)
    scores = [
        [dot(k[:, head_cols(h)], q_ref[:, head_cols(h)], 1, 1) for k in (ko_ref, kr_ref)]
        for h in heads
    ]
    expos = []
    for h in heads:
        top = jnp.maximum(
            jnp.max(scores[h][0], axis=0, keepdims=True),
            jnp.max(scores[h][1], axis=0, keepdims=True),
        )
        shift = top * EXP2_SCALE
        expo = [jnp.exp2(s * EXP2_SCALE - shift) for s in scores[h]]
        den = jnp.sum(expo[0], axis=0, keepdims=True) + jnp.sum(expo[1], axis=0, keepdims=True)
        expos.append(([e.astype(BF16) for e in expo], den))
        lse_ref[h : h + 1, :] = top * SCALE + jnp.log(den)
    for h in heads:
        (own, other), den = expos[h]
        num = dot(vo_ref[:, head_cols(h)], own, 0, 0) + dot(vr_ref[:, head_cols(h)], other, 0, 0)
        part_ref[:, head_cols(h)] = jnp.transpose(num / den).astype(BF16)


def forward(place, queries, keys, keys_in, values, values_in):
    tokens = keys.shape[0]
    block = 512
    own = pl.BlockSpec((tokens, WIDE), lambda i, c: (0, c[0]))
    grid_spec = pltpu.PrefetchScalarGridSpec(
        num_scalar_prefetch=1,
        grid=(LATENTS // block,),
        in_specs=[
            pl.BlockSpec((block, WIDE), lambda i, c: (i, c[0])),
            own, own, own, own,
        ],
        out_specs=[
            pl.BlockSpec((block, WIDE), lambda i, c: (i, 0)),
            pl.BlockSpec((8, block), lambda i, c: (0, i)),
        ],
    )
    return pl.pallas_call(
        forward_kernel,
        out_shape=[
            jax.ShapeDtypeStruct((LATENTS, WIDE), BF16),
            jax.ShapeDtypeStruct((8, LATENTS), F32),
        ],
        grid_spec=grid_spec,
        compiler_params=params(60),
        cost_estimate=pl.CostEstimate(
            flops=9_000_000_000, bytes_accessed=4_000_000, transcendentals=4_194_304
        ),
        name="forward",
    )(place, queries, keys, keys_in, values, values_in)


def message_kernel(part_ref, lse_ref, dout_ref, msg_ref, stat_ref):
    rows = []
    deltas = []
    stat_ref[...] = jnp.zeros_like(stat_ref)
    for h in range(HEADS_HERE):
        cols = head_cols(h)
        dout = dout_ref[:, :, cols].reshape(LATENTS, HDIM).astype(F32)
        delta = jnp.sum(part_ref[:, cols].astype(F32) * dout, axis=1, keepdims=True)
        deltas.append(jnp.transpose(jnp.broadcast_to(delta, (LATENTS, HDIM)))[0:1, :])
        stat_ref[h : h + 1, :] = lse_ref[h : h + 1, :] * LOG2E
        stat_ref[2 + h : 3 + h, :] = deltas[h]
    for h in range(HEADS_HERE):
        rows.extend(in_three(lse_ref[h : h + 1, :]))
    for h in range(HEADS_HERE):
        rows.extend(in_three(deltas[h]))
    stats = jnp.concatenate(rows, axis=0)
    stats = jnp.concatenate([stats[:, i * WIDE : (i + 1) * WIDE] for i in range(4)], axis=0)
    for c in range(N_CHIPS):
        msg_ref[c, 0:NUM, :] = part_ref[c * NUM : (c + 1) * NUM, :]
        msg_ref[c, NUM:, :] = stats


def message(part, lse, dout):
    return pl.pallas_call(
        message_kernel,
        out_shape=[
            jax.ShapeDtypeStruct((N_CHIPS, ROWS1, WIDE), BF16),
            jax.ShapeDtypeStruct((8, LATENTS), F32),
        ],
        grid=(1,),
        in_specs=[whole(LATENTS, WIDE), whole(8, LATENTS), whole(N_CHIPS, NUM, WIDE)],
        out_specs=[whole(N_CHIPS, ROWS1, WIDE), whole(8, LATENTS)],
        compiler_params=params(60),
        name="message",
    )(part, lse, dout)


def combine_kernel(
    place_ref, msg_ref, own_ref, a_ref, b_ref, att_ref, stat_ref, out_ref
):
    y = place_ref[1]
    zh = place_ref[2]
    mine = [jnp.zeros((N_CHIPS, WIDE), F32) for _ in range(HEADS_HERE)]
    stat_ref[...] = jnp.zeros_like(stat_ref)
    for i in range(4):
        blocks = [msg_ref[c, NUM:, :].astype(F32) for c in range(N_CHIPS)]
        cols = slice(i * WIDE, (i + 1) * WIDE)

        def value(r):
            at = 12 * i + 3 * r
            return jnp.concatenate(
                [b[at : at + 1] + b[at + 1 : at + 2] + b[at + 2 : at + 3] for b in blocks], axis=0
            )

        for h in range(HEADS_HERE):
            lse = value(h)
            delta = value(2 + h)
            top = jnp.max(lse, axis=0, keepdims=True)
            total = top + jnp.log(jnp.sum(jnp.exp(lse - top), axis=0, keepdims=True))
            weight = jnp.exp(lse - total)
            stat_ref[h : h + 1, cols] = total * LOG2E
            stat_ref[2 + h : 3 + h, cols] = jnp.sum(weight * delta, axis=0, keepdims=True)
            mine[h] = jnp.where(y == i, weight, mine[h])
    att_all = []
    for h in range(HEADS_HERE):
        rows = jnp.zeros((N_CHIPS, NUM), F32)
        for z in range(4):
            rows = jnp.where(zh == z, mine[h][:, z * NUM : (z + 1) * NUM], rows)
        weight = jnp.transpose(rows)
        att = jnp.zeros((NUM, HDIM), F32)
        for c in range(N_CHIPS):
            att = att + msg_ref[c, 0:NUM, head_cols(h)].astype(F32) * weight[:, c : c + 1]
        att_all.append(att.astype(BF16))
    att = jnp.concatenate(att_all, axis=1)
    att_ref[...] = att
    for c in range(N_CHIPS):
        out_ref[c, NUM:, :] = att
    for h in range(HEADS_HERE):
        cols = head_cols(h)
        share = jnp.exp2(own_ref[h : h + 1, :] - stat_ref[h : h + 1, :]) * SCALE
        rest = stat_ref[2 + h : 3 + h, :] - own_ref[2 + h : 3 + h, :]
        dq = jnp.transpose(share * (a_ref[cols, :].astype(F32) - rest * b_ref[cols, :].astype(F32))).astype(BF16)
        out_ref[:, 0:NUM, cols] = dq.reshape(N_CHIPS, NUM, HDIM)


def combine(place, msg, own_stats, a, b):
    grid_spec = pltpu.PrefetchScalarGridSpec(
        num_scalar_prefetch=1,
        grid=(1,),
        in_specs=[
            whole(N_CHIPS, ROWS1, WIDE), whole(8, LATENTS),
            whole(WIDE, LATENTS), whole(WIDE, LATENTS),
        ],
        out_specs=[whole(NUM, WIDE), whole(8, LATENTS), whole(N_CHIPS, ROWS2, WIDE)],
    )
    return pl.pallas_call(
        combine_kernel,
        out_shape=[
            jax.ShapeDtypeStruct((NUM, WIDE), BF16),
            jax.ShapeDtypeStruct((8, LATENTS), F32),
            jax.ShapeDtypeStruct((N_CHIPS, ROWS2, WIDE), BF16),
        ],
        grid_spec=grid_spec,
        compiler_params=params(24),
        name="combine",
    )(place, msg, own_stats, a, b)


def query_kernel(
    place_ref, q_ref, dout_ref, stat_ref, ko_ref, kr_ref, vo_ref, vr_ref,
    a_ref, b_ref, prob_ref,
):
    h = pl.program_id(0)
    block = 256
    for at in range(0, LATENTS, block):
        rows = slice(at, at + block)
        q = q_ref[rows, :]
        dout = dout_ref[at // NUM : (at + block) // NUM].reshape(block, HDIM)
        lse = stat_ref[pl.ds(h, 1), rows]
        delta = stat_ref[pl.ds(2 + h, 1), rows]
        a = 0
        b = 0
        for src, (k_ref, v_ref) in enumerate(((ko_ref, vo_ref), (kr_ref, vr_ref))):
            k = k_ref[...]
            probs = jnp.exp2(dot(k, q, 1, 1) * EXP2_SCALE - lse)
            dscore = (probs * (dot(v_ref[...], dout, 1, 1) - delta)).astype(BF16)
            probs = probs.astype(BF16)
            prob_ref[0, src, :, rows] = probs
            a = a + dot(k, dscore, 0, 0)
            b = b + dot(k, probs, 0, 0)
        a_ref[:, rows] = a.astype(BF16)
        b_ref[:, rows] = b.astype(BF16)


def query_parts(place, queries, dout, stats, keys, keys_in, values, values_in):
    tokens = keys.shape[0]
    head = pl.BlockSpec((tokens, HDIM), lambda h, c: (0, c[0] * HEADS_HERE + h))
    sums = pl.BlockSpec((HDIM, LATENTS), lambda h, c: (h, 0))
    kept = pl.BlockSpec((1, 2, tokens, LATENTS), lambda h, c: (h, 0, 0, 0))
    grid_spec = pltpu.PrefetchScalarGridSpec(
        num_scalar_prefetch=1,
        grid=(HEADS_HERE,),
        in_specs=[
            pl.BlockSpec((LATENTS, HDIM), lambda h, c: (0, c[0] * HEADS_HERE + h)),
            pl.BlockSpec((N_CHIPS, NUM, HDIM), lambda h, c: (0, 0, h)),
            whole(8, LATENTS),
            head, head, head, head,
        ],
        out_specs=[sums, sums, kept],
    )
    return pl.pallas_call(
        query_kernel,
        out_shape=[
            jax.ShapeDtypeStruct((WIDE, LATENTS), BF16),
            jax.ShapeDtypeStruct((WIDE, LATENTS), BF16),
            jax.ShapeDtypeStruct((HEADS_HERE, 2, tokens, LATENTS), BF16),
        ],
        grid_spec=grid_spec,
        compiler_params=params(60),
        cost_estimate=pl.CostEstimate(
            flops=12_000_000_000, bytes_accessed=20_000_000, transcendentals=4_194_304
        ),
        name="query",
    )(place, queries, dout, stats, keys, keys_in, values, values_in)


def token_kernel(
    place_ref, q_ref, dout_ref, own_ref, stat_ref, prob_ref, vo_ref, vr_ref,
    dko_ref, dkr_ref, dvo_ref, dvr_ref, dout_scaled_ref, q_scaled_ref,
):
    h = pl.program_id(0)

    @pl.when(pl.program_id(1) == 0)
    def _():
        share = jnp.exp2(own_ref[pl.ds(h, 1), :] - stat_ref[pl.ds(h, 1), :])
        share = jnp.transpose(jnp.broadcast_to(share, (HDIM, LATENTS)))
        dout = dout_ref[...].reshape(LATENTS, HDIM).astype(F32)
        dout_scaled_ref[...] = (share * dout).astype(BF16)
        q_scaled_ref[...] = (share * q_ref[...].astype(F32)).astype(BF16)

    delta = stat_ref[pl.ds(2 + h, 1), :]
    dout = dout_ref[...].reshape(LATENTS, HDIM)
    dprobs = [dot(v_ref[...], dout, 1, 1) for v_ref in (vo_ref, vr_ref)]
    dv = [dot(prob_ref[0, src], dout_scaled_ref[...], 1, 0) for src in (0, 1)]
    dscores = [
        (prob_ref[0, src].astype(F32) * (dprobs[src] - delta)).astype(BF16) for src in (0, 1)
    ]
    dk = [dot(dscores[src], q_scaled_ref[...], 1, 0) for src in (0, 1)]
    for src, (dk_ref, dv_ref) in enumerate(((dko_ref, dvo_ref), (dkr_ref, dvr_ref))):
        dv_ref[...] = dv[src].astype(BF16)
        dk_ref[...] = (dk[src] * SCALE).astype(BF16)


def token_grads(place, queries, dout, own_stats, stats, probs, values, values_in):
    tokens = probs.shape[2]
    block = 512
    own = pl.BlockSpec((block, HDIM), lambda h, i, c: (i, c[0] * HEADS_HERE + h))
    other = pl.BlockSpec((block, HDIM), lambda h, i, c: (i, h))
    kept = pl.BlockSpec((1, 2, block, LATENTS), lambda h, i, c: (h, 0, i, 0))
    grid_spec = pltpu.PrefetchScalarGridSpec(
        num_scalar_prefetch=1,
        grid=(HEADS_HERE, tokens // block),
        in_specs=[
            pl.BlockSpec((LATENTS, HDIM), lambda h, i, c: (0, c[0] * HEADS_HERE + h)),
            pl.BlockSpec((N_CHIPS, NUM, HDIM), lambda h, i, c: (0, 0, h)),
            whole(8, LATENTS),
            whole(8, LATENTS),
            kept, own, own,
        ],
        out_specs=[own, other, own, other],
        scratch_shapes=[pltpu.VMEM((LATENTS, HDIM), BF16), pltpu.VMEM((LATENTS, HDIM), BF16)],
    )
    full = jax.ShapeDtypeStruct((tokens, 2 * WIDE), BF16)
    half_wide = jax.ShapeDtypeStruct((tokens, WIDE), BF16)
    return pl.pallas_call(
        token_kernel,
        out_shape=[full, half_wide, full, half_wide],
        grid_spec=grid_spec,
        compiler_params=params(60),
        cost_estimate=pl.CostEstimate(
            flops=8_000_000_000, bytes_accessed=14_000_000, transcendentals=0
        ),
        name="token",
    )(place, queries, dout, own_stats, stats, probs, values, values_in)


def weight_kernel(place_ref, att_ref, own_ref, other_ref, out_ref, cot_ref):
    core = place_ref[0]
    cot_ref[:, pl.ds(pl.multiple_of(core * COT, COT), COT), :] = own_ref[...]
    cot_ref[:, pl.ds(pl.multiple_of((1 - core) * COT, COT), COT), :] = other_ref[...]
    att = att_ref[...].reshape(LATENTS, WIDE)
    cot = cot_ref[...].reshape(LATENTS, WIDE)
    out_ref[...] = dot(att, cot, 0, 0)


def weight(place, msg, cot, cot_in):
    grid_spec = pltpu.PrefetchScalarGridSpec(
        num_scalar_prefetch=1,
        grid=(1,),
        in_specs=[
            pl.BlockSpec((N_CHIPS, NUM, WIDE), lambda i, c: (0, 1, 0)),
            whole(N_CHIPS, COT, WIDE),
            whole(N_CHIPS, COT, WIDE),
        ],
        out_specs=whole(WIDE, WIDE),
        scratch_shapes=[pltpu.VMEM((N_CHIPS, NUM, WIDE), BF16)],
    )
    return pl.pallas_call(
        weight_kernel,
        out_shape=jax.ShapeDtypeStruct((WIDE, WIDE), F32),
        grid_spec=grid_spec,
        compiler_params=params(24),
        name="weight",
    )(place, msg, cot, cot_in)


def swap(x):
    return lax.ppermute(x, "core", [(0, 1), (1, 0)])


def half(x, index, axis):
    size = x.shape[axis] // 2
    return lax.dynamic_slice_in_dim(x, index * size, size, axis)


def in_order(core, mine, other, axis):
    return jnp.where(
        core == 0,
        jnp.concatenate([mine, other], axis),
        jnp.concatenate([other, mine], axis),
    )


def gather(x, axes, size):
    tiled = jnp.broadcast_to(x[None], (size,) + x.shape)
    return lax.all_to_all(tiled, axes, 0, 0, tiled=True)


def shift(x, axis, d):
    return lax.ppermute(x, axis, [(i, (i + d) % 4) for i in range(4)])


def after(x, *others):
    return lax.optimization_barrier((x,) + others)[0]


def body(queries, prefix_keys, prefix_values, out_weight, out_grad):
    core = lax.axis_index("core")
    at_x, at_zl = lax.axis_index("x"), lax.axis_index("zl")
    odd_x = lax.rem(at_x, 2)
    place = jnp.stack([core, lax.axis_index("y"), lax.axis_index("zh"), odd_x]).astype(jnp.int32)
    cot = gather(out_grad, TP, 8)
    keys_in = swap(prefix_keys)
    values_in = swap(prefix_values)
    cot, keys_in, values_in = lax.optimization_barrier((cot, keys_in, values_in))
    tokens = (prefix_keys, keys_in, prefix_values, values_in)

    dout = dout_rows(place, cot, swap(cot), out_weight)
    dout = lax.all_to_all(dout, CHIPS, 0, 0, tiled=True)
    part, lse = forward(place, queries, *tokens)
    msg1, own_stats = message(part, lse, dout)
    msg1 = lax.all_to_all(msg1, CHIPS, 0, 0, tiled=True)
    cot_part = dout[:, NUM:]
    cot_other = lax.ppermute(cot_part, "x", [(0, 1), (1, 0), (2, 3), (3, 2)])
    cot_mine = in_order(odd_x, cot_part, cot_other, 1)
    cot_in = swap(cot_mine)
    a, b, probs = query_parts(place, queries, dout, own_stats, *tokens)

    msg1, cot_mine, cot_in = lax.optimization_barrier((msg1, cot_mine, cot_in))
    att64, stats, msg2 = combine(place, msg1, own_stats, a, b)
    msg2 = lax.all_to_all(msg2, CHIPS, 0, 0, tiled=True)

    att32 = in_order(core, half(att64, core, 0), swap(half(att64, 1 - core, 0)), 1)
    partial_out = dot(att32, out_weight, 1, 0).reshape(32, 4, 1024).transpose(1, 0, 2)
    by_x = [
        lax.dynamic_index_in_dim(partial_out, lax.rem(at_x + d, 4), 0, keepdims=False)
        for d in range(4)
    ]
    from_x = [shift(by_x[d].astype(BF16), "x", d) for d in (1, 2, 3)]
    dk, dk_out, dv, dv_out = token_grads(
        place, queries, dout, own_stats, after(stats, by_x[0]), probs, prefix_values, values_in
    )
    own_x, *from_x = lax.optimization_barrier((by_x[0], *from_x, dk))[:4]
    over_x = own_x + sum(x.astype(F32) for x in from_x)
    by_zl = over_x.reshape(32, 2, 512).transpose(1, 0, 2)
    from_zl = lax.ppermute(
        lax.dynamic_index_in_dim(by_zl, 1 - at_zl, 0, keepdims=False).astype(BF16),
        "zl",
        [(0, 1), (1, 0)],
    )
    own_zl = lax.dynamic_index_in_dim(by_zl, at_zl, 0, keepdims=False)
    other_cols = (jnp.int32(0), ((1 - core) * WIDE).astype(jnp.int32))
    key_grad = lax.dynamic_update_slice(dk, swap(dk_out), other_cols)
    value_grad = lax.dynamic_update_slice(dv, swap(dv_out), other_cols)

    msg2, from_zl = lax.optimization_barrier((msg2, from_zl, key_grad, value_grad))[:2]
    latent_out = (own_zl + from_zl.astype(F32)).astype(BF16)
    dq64 = jnp.sum(msg2[:, :NUM].astype(F32), axis=0).astype(BF16)
    dq_in = swap(half(dq64, 1 - core, 0))
    query_grad = in_order(core, half(dq64, core, 0), dq_in, 1)
    weight_part = weight(place, msg2, cot_mine, cot_in)
    weight_in = swap(half(weight_part, 1 - core, 1))
    weight_grad = in_order(core, half(weight_part, core, 1), weight_in, 0)
    return latent_out, query_grad, key_grad, value_grad, weight_grad


def solution(mesh):
    fine = Mesh(mesh.devices.reshape(4, 4, 2, 4, 2), ("y", "zh", "core", "x", "zl"))
    placed = (P(None, TP), P(CTX, TP), P(CTX, TP), P(TP, None), P(CTX, TP))
    return jax.shard_map(
        body,
        mesh=fine,
        in_specs=placed,
        out_specs=(P(CTX, TP), P(CTX, TP), P(CTX, TP), P(CTX, TP), P(TP, CTX)),
        check_vma=False,
    )
```

```python
import math

import jax
import jax.numpy as jnp
from jax import lax
from jax.experimental import pallas as pl
from jax.experimental.pallas import tpu as pltpu
from jax.sharding import Mesh
from jax.sharding import PartitionSpec as P

HDIM = 128
SCALE = HDIM ** (-0.5)
LOG2E = math.log2(math.e)
EXP2_SCALE = SCALE * LOG2E
CHIPS = ("y", "zh")
CTX = ("y", "zh", "core")
TP = ("x", "zl")
N_CHIPS = 16
HEADS_HERE = 2
WIDE = HEADS_HERE * HDIM
NUM, STAT, COT, PART = 64, 48, 32, 16
ROWS1 = NUM + STAT
ROWS2 = NUM + NUM
ROWS0 = NUM + PART
LATENTS = N_CHIPS * NUM
F32 = jnp.float32
BF16 = jnp.bfloat16


def dot(a, b, ca, cb):
    return lax.dot_general(a, b, (((ca,), (cb,)), ((), ())), preferred_element_type=F32)


def in_three(x):
    high = x.astype(BF16)
    rest = x - high.astype(F32)
    middle = rest.astype(BF16)
    low = (rest - middle.astype(F32)).astype(BF16)
    return high, middle, low


def params(mib):
    return pltpu.CompilerParams(vmem_limit_bytes=mib * 1024 * 1024)


def whole(*shape):
    return pl.BlockSpec(shape, lambda *_: (0,) * len(shape))


def head_cols(h):
    return slice(h * HDIM, (h + 1) * HDIM)


def dout_kernel(place_ref, own_ref, other_ref, w_ref, out_ref, cot_ref):
    core = place_ref[0]
    for row, ref in ((core, own_ref), (1 - core, other_ref)):
        start = pl.multiple_of(row * COT, COT)
        for b in range(8):
            cot_ref[pl.ds(start, COT), b * 512 : (b + 1) * 512] = ref[b]
    dout = jnp.transpose(dot(w_ref[...], cot_ref[...], 1, 1)).astype(BF16)
    start = pl.multiple_of(core * COT + place_ref[3] * PART, PART)
    for c in range(N_CHIPS):
        out_ref[c, 0:NUM, :] = dout
        out_ref[c, NUM:, :] = cot_ref[pl.ds(start, PART), c * WIDE : (c + 1) * WIDE]


def dout_rows(place, cot, cot_in, out_weight):
    depth = out_weight.shape[1]
    grid_spec = pltpu.PrefetchScalarGridSpec(
        num_scalar_prefetch=1,
        grid=(1,),
        in_specs=[
            whole(8, COT, 512),
            whole(8, COT, 512),
            pl.BlockSpec((WIDE, depth), lambda i, c: (c[0], 0)),
        ],
        out_specs=whole(N_CHIPS, ROWS0, WIDE),
        scratch_shapes=[pltpu.VMEM((NUM, depth), BF16)],
    )
    return pl.pallas_call(
        dout_kernel,
        out_shape=jax.ShapeDtypeStruct((N_CHIPS, ROWS0, WIDE), BF16),
        grid_spec=grid_spec,
        compiler_params=params(60),
        name="dout",
    )(place, cot, cot_in, out_weight)


def forward_kernel(place_ref, q_ref, ko_ref, kr_ref, vo_ref, vr_ref, part_ref, lse_ref):
    heads = range(HEADS_HERE)
    scores = [
        [dot(k[:, head_cols(h)], q_ref[:, head_cols(h)], 1, 1) for k in (ko_ref, kr_ref)]
        for h in heads
    ]
    expos = []
    for h in heads:
        top = jnp.maximum(
            jnp.max(scores[h][0], axis=0, keepdims=True),
            jnp.max(scores[h][1], axis=0, keepdims=True),
        )
        shift = top * EXP2_SCALE
        expo = [jnp.exp2(s * EXP2_SCALE - shift) for s in scores[h]]
        den = jnp.sum(expo[0], axis=0, keepdims=True) + jnp.sum(expo[1], axis=0, keepdims=True)
        expos.append(([e.astype(BF16) for e in expo], den))
        lse_ref[h : h + 1, :] = top * SCALE + jnp.log(den)
    for h in heads:
        (own, other), den = expos[h]
        num = dot(vo_ref[:, head_cols(h)], own, 0, 0) + dot(vr_ref[:, head_cols(h)], other, 0, 0)
        part_ref[:, head_cols(h)] = jnp.transpose(num / den).astype(BF16)


def forward(place, queries, keys, keys_in, values, values_in):
    tokens = keys.shape[0]
    block = 512
    own = pl.BlockSpec((tokens, WIDE), lambda i, c: (0, c[0]))
    grid_spec = pltpu.PrefetchScalarGridSpec(
        num_scalar_prefetch=1,
        grid=(LATENTS // block,),
        in_specs=[
            pl.BlockSpec((block, WIDE), lambda i, c: (i, c[0])),
            own, own, own, own,
        ],
        out_specs=[
            pl.BlockSpec((block, WIDE), lambda i, c: (i, 0)),
            pl.BlockSpec((8, block), lambda i, c: (0, i)),
        ],
    )
    return pl.pallas_call(
        forward_kernel,
        out_shape=[
            jax.ShapeDtypeStruct((LATENTS, WIDE), BF16),
            jax.ShapeDtypeStruct((8, LATENTS), F32),
        ],
        grid_spec=grid_spec,
        compiler_params=params(60),
        cost_estimate=pl.CostEstimate(
            flops=9_000_000_000, bytes_accessed=4_000_000, transcendentals=4_194_304
        ),
        name="forward",
    )(place, queries, keys, keys_in, values, values_in)


def message_kernel(part_ref, lse_ref, dout_ref, msg_ref, stat_ref):
    rows = []
    deltas = []
    stat_ref[...] = jnp.zeros_like(stat_ref)
    for h in range(HEADS_HERE):
        cols = head_cols(h)
        dout = dout_ref[:, :, cols].reshape(LATENTS, HDIM).astype(F32)
        delta = jnp.sum(part_ref[:, cols].astype(F32) * dout, axis=1, keepdims=True)
        deltas.append(jnp.transpose(jnp.broadcast_to(delta, (LATENTS, HDIM)))[0:1, :])
        stat_ref[h : h + 1, :] = lse_ref[h : h + 1, :] * LOG2E
        stat_ref[2 + h : 3 + h, :] = deltas[h]
    for h in range(HEADS_HERE):
        rows.extend(in_three(lse_ref[h : h + 1, :]))
    for h in range(HEADS_HERE):
        rows.extend(in_three(deltas[h]))
    stats = jnp.concatenate(rows, axis=0)
    stats = jnp.concatenate([stats[:, i * WIDE : (i + 1) * WIDE] for i in range(4)], axis=0)
    for c in range(N_CHIPS):
        msg_ref[c, 0:NUM, :] = part_ref[c * NUM : (c + 1) * NUM, :]
        msg_ref[c, NUM:, :] = stats


def message(part, lse, dout):
    return pl.pallas_call(
        message_kernel,
        out_shape=[
            jax.ShapeDtypeStruct((N_CHIPS, ROWS1, WIDE), BF16),
            jax.ShapeDtypeStruct((8, LATENTS), F32),
        ],
        grid=(1,),
        in_specs=[whole(LATENTS, WIDE), whole(8, LATENTS), whole(N_CHIPS, NUM, WIDE)],
        out_specs=[whole(N_CHIPS, ROWS1, WIDE), whole(8, LATENTS)],
        compiler_params=params(60),
        name="message",
    )(part, lse, dout)


def combine_kernel(
    place_ref, msg_ref, own_ref, sums_ref, att_ref, stat_ref, out_ref
):
    y = place_ref[1]
    zh = place_ref[2]
    mine = [jnp.zeros((N_CHIPS, WIDE), F32) for _ in range(HEADS_HERE)]
    stat_ref[...] = jnp.zeros_like(stat_ref)
    for i in range(4):
        blocks = [msg_ref[c, NUM:, :].astype(F32) for c in range(N_CHIPS)]
        cols = slice(i * WIDE, (i + 1) * WIDE)

        def value(r):
            at = 12 * i + 3 * r
            return jnp.concatenate(
                [b[at : at + 1] + b[at + 1 : at + 2] + b[at + 2 : at + 3] for b in blocks], axis=0
            )

        for h in range(HEADS_HERE):
            lse = value(h)
            delta = value(2 + h)
            top = jnp.max(lse, axis=0, keepdims=True)
            total = top + jnp.log(jnp.sum(jnp.exp(lse - top), axis=0, keepdims=True))
            weight = jnp.exp(lse - total)
            stat_ref[h : h + 1, cols] = total * LOG2E
            stat_ref[2 + h : 3 + h, cols] = jnp.sum(weight * delta, axis=0, keepdims=True)
            mine[h] = jnp.where(y == i, weight, mine[h])
    att_all = []
    for h in range(HEADS_HERE):
        rows = jnp.zeros((N_CHIPS, NUM), F32)
        for z in range(4):
            rows = jnp.where(zh == z, mine[h][:, z * NUM : (z + 1) * NUM], rows)
        weight = jnp.transpose(rows)
        att = jnp.zeros((NUM, HDIM), F32)
        for c in range(N_CHIPS):
            att = att + msg_ref[c, 0:NUM, head_cols(h)].astype(F32) * weight[:, c : c + 1]
        att_all.append(att.astype(BF16))
    att = jnp.concatenate(att_all, axis=1)
    att_ref[...] = att
    for c in range(N_CHIPS):
        out_ref[c, NUM:, :] = att
    for h in range(HEADS_HERE):
        cols = head_cols(h)
        share = jnp.exp2(own_ref[h : h + 1, :] - stat_ref[h : h + 1, :]) * SCALE
        rest = stat_ref[2 + h : 3 + h, :] - own_ref[2 + h : 3 + h, :]
        at_scores = sums_ref[0, cols, :].astype(F32)
        at_probs = sums_ref[1, cols, :].astype(F32)
        dq = jnp.transpose(share * (at_scores - rest * at_probs)).astype(BF16)
        out_ref[:, 0:NUM, cols] = dq.reshape(N_CHIPS, NUM, HDIM)


def combine(place, msg, own_stats, sums):
    grid_spec = pltpu.PrefetchScalarGridSpec(
        num_scalar_prefetch=1,
        grid=(1,),
        in_specs=[
            whole(N_CHIPS, ROWS1, WIDE), whole(8, LATENTS),
            whole(2, WIDE, LATENTS),
        ],
        out_specs=[whole(NUM, WIDE), whole(8, LATENTS), whole(N_CHIPS, ROWS2, WIDE)],
    )
    return pl.pallas_call(
        combine_kernel,
        out_shape=[
            jax.ShapeDtypeStruct((NUM, WIDE), BF16),
            jax.ShapeDtypeStruct((8, LATENTS), F32),
            jax.ShapeDtypeStruct((N_CHIPS, ROWS2, WIDE), BF16),
        ],
        grid_spec=grid_spec,
        compiler_params=params(24),
        name="combine",
    )(place, msg, own_stats, sums)


def query_kernel(
    place_ref, q_ref, dout_ref, stat_ref, ko_ref, kr_ref, vo_ref, vr_ref,
    sums_ref, prob_ref,
):
    h = pl.program_id(0)
    block = 256
    for at in range(0, LATENTS, block):
        rows = slice(at, at + block)
        q = q_ref[rows, :]
        dout = dout_ref[at // NUM : (at + block) // NUM].reshape(block, HDIM)
        lse = stat_ref[pl.ds(h, 1), rows]
        delta = stat_ref[pl.ds(2 + h, 1), rows]
        a = 0
        b = 0
        for src, (k_ref, v_ref) in enumerate(((ko_ref, vo_ref), (kr_ref, vr_ref))):
            k = k_ref[...]
            probs = jnp.exp2(dot(k, q, 1, 1) * EXP2_SCALE - lse)
            dscore = (probs * (dot(v_ref[...], dout, 1, 1) - delta)).astype(BF16)
            probs = probs.astype(BF16)
            prob_ref[0, src, :, rows] = probs
            a = a + dot(k, dscore, 0, 0)
            b = b + dot(k, probs, 0, 0)
        sums_ref[0, :, rows] = a.astype(BF16)
        sums_ref[1, :, rows] = b.astype(BF16)


def query_parts(place, queries, dout, stats, keys, keys_in, values, values_in):
    tokens = keys.shape[0]
    head = pl.BlockSpec((tokens, HDIM), lambda h, c: (0, c[0] * HEADS_HERE + h))
    sums = pl.BlockSpec((2, HDIM, LATENTS), lambda h, c: (0, h, 0))
    kept = pl.BlockSpec((1, 2, tokens, LATENTS), lambda h, c: (h, 0, 0, 0))
    grid_spec = pltpu.PrefetchScalarGridSpec(
        num_scalar_prefetch=1,
        grid=(HEADS_HERE,),
        in_specs=[
            pl.BlockSpec((LATENTS, HDIM), lambda h, c: (0, c[0] * HEADS_HERE + h)),
            pl.BlockSpec((N_CHIPS, NUM, HDIM), lambda h, c: (0, 0, h)),
            whole(8, LATENTS),
            head, head, head, head,
        ],
        out_specs=[sums, kept],
    )
    return pl.pallas_call(
        query_kernel,
        out_shape=[
            jax.ShapeDtypeStruct((2, WIDE, LATENTS), BF16),
            jax.ShapeDtypeStruct((HEADS_HERE, 2, tokens, LATENTS), BF16),
        ],
        grid_spec=grid_spec,
        compiler_params=params(60),
        cost_estimate=pl.CostEstimate(
            flops=12_000_000_000, bytes_accessed=20_000_000, transcendentals=4_194_304
        ),
        name="query",
    )(place, queries, dout, stats, keys, keys_in, values, values_in)


def token_kernel(
    place_ref, q_ref, dout_ref, own_ref, stat_ref, prob_ref, vo_ref, vr_ref,
    dko_ref, dkr_ref, dvo_ref, dvr_ref, dout_scaled_ref, q_scaled_ref,
):
    h = pl.program_id(0)

    @pl.when(pl.program_id(1) == 0)
    def _():
        share = jnp.exp2(own_ref[pl.ds(h, 1), :] - stat_ref[pl.ds(h, 1), :])
        share = jnp.transpose(jnp.broadcast_to(share, (HDIM, LATENTS)))
        dout = dout_ref[...].reshape(LATENTS, HDIM).astype(F32)
        dout_scaled_ref[...] = (share * dout).astype(BF16)
        q_scaled_ref[...] = (share * q_ref[...].astype(F32)).astype(BF16)

    delta = stat_ref[pl.ds(2 + h, 1), :]
    dout = dout_ref[...].reshape(LATENTS, HDIM)
    dprobs = [dot(v_ref[...], dout, 1, 1) for v_ref in (vo_ref, vr_ref)]
    dv = [dot(prob_ref[0, src], dout_scaled_ref[...], 1, 0) for src in (0, 1)]
    dscores = [
        (prob_ref[0, src].astype(F32) * (dprobs[src] - delta)).astype(BF16) for src in (0, 1)
    ]
    dk = [dot(dscores[src], q_scaled_ref[...], 1, 0) for src in (0, 1)]
    for src, (dk_ref, dv_ref) in enumerate(((dko_ref, dvo_ref), (dkr_ref, dvr_ref))):
        dv_ref[...] = dv[src].astype(BF16)
        dk_ref[...] = (dk[src] * SCALE).astype(BF16)


def token_grads(place, queries, dout, own_stats, stats, probs, values, values_in):
    tokens = probs.shape[2]
    block = 512
    own = pl.BlockSpec((block, HDIM), lambda h, i, c: (i, c[0] * HEADS_HERE + h))
    other = pl.BlockSpec((block, HDIM), lambda h, i, c: (i, h))
    kept = pl.BlockSpec((1, 2, block, LATENTS), lambda h, i, c: (h, 0, i, 0))
    grid_spec = pltpu.PrefetchScalarGridSpec(
        num_scalar_prefetch=1,
        grid=(HEADS_HERE, tokens // block),
        in_specs=[
            pl.BlockSpec((LATENTS, HDIM), lambda h, i, c: (0, c[0] * HEADS_HERE + h)),
            pl.BlockSpec((N_CHIPS, NUM, HDIM), lambda h, i, c: (0, 0, h)),
            whole(8, LATENTS),
            whole(8, LATENTS),
            kept, own, own,
        ],
        out_specs=[own, other, own, other],
        scratch_shapes=[pltpu.VMEM((LATENTS, HDIM), BF16), pltpu.VMEM((LATENTS, HDIM), BF16)],
    )
    full = jax.ShapeDtypeStruct((tokens, 2 * WIDE), BF16)
    half_wide = jax.ShapeDtypeStruct((tokens, WIDE), BF16)
    return pl.pallas_call(
        token_kernel,
        out_shape=[full, half_wide, full, half_wide],
        grid_spec=grid_spec,
        compiler_params=params(60),
        cost_estimate=pl.CostEstimate(
            flops=8_000_000_000, bytes_accessed=14_000_000, transcendentals=0
        ),
        name="token",
    )(place, queries, dout, own_stats, stats, probs, values, values_in)


def weight_kernel(place_ref, att_ref, own_ref, other_ref, out_ref, cot_ref):
    core = place_ref[0]
    cot_ref[:, pl.ds(pl.multiple_of(core * COT, COT), COT), :] = own_ref[...]
    cot_ref[:, pl.ds(pl.multiple_of((1 - core) * COT, COT), COT), :] = other_ref[...]
    att = att_ref[...].reshape(LATENTS, WIDE)
    cot = cot_ref[...].reshape(LATENTS, WIDE)
    out_ref[...] = dot(att, cot, 0, 0)


def weight(place, msg, cot, cot_in):
    grid_spec = pltpu.PrefetchScalarGridSpec(
        num_scalar_prefetch=1,
        grid=(1,),
        in_specs=[
            pl.BlockSpec((N_CHIPS, NUM, WIDE), lambda i, c: (0, 1, 0)),
            whole(N_CHIPS, COT, WIDE),
            whole(N_CHIPS, COT, WIDE),
        ],
        out_specs=whole(WIDE, WIDE),
        scratch_shapes=[pltpu.VMEM((N_CHIPS, NUM, WIDE), BF16)],
    )
    return pl.pallas_call(
        weight_kernel,
        out_shape=jax.ShapeDtypeStruct((WIDE, WIDE), F32),
        grid_spec=grid_spec,
        compiler_params=params(24),
        name="weight",
    )(place, msg, cot, cot_in)


def swap(x):
    return lax.ppermute(x, "core", [(0, 1), (1, 0)])


def half(x, index, axis):
    size = x.shape[axis] // 2
    return lax.dynamic_slice_in_dim(x, index * size, size, axis)


def in_order(core, mine, other, axis):
    return jnp.where(
        core == 0,
        jnp.concatenate([mine, other], axis),
        jnp.concatenate([other, mine], axis),
    )


def gather(x, axes, size):
    tiled = jnp.broadcast_to(x[None], (size,) + x.shape)
    return lax.all_to_all(tiled, axes, 0, 0, tiled=True)


def shift(x, axis, d):
    return lax.ppermute(x, axis, [(i, (i + d) % 4) for i in range(4)])


def after(x, *others):
    return lax.optimization_barrier((x,) + others)[0]


def body(queries, prefix_keys, prefix_values, out_weight, out_grad):
    core = lax.axis_index("core")
    at_x, at_zl = lax.axis_index("x"), lax.axis_index("zl")
    odd_x = lax.rem(at_x, 2)
    place = jnp.stack([core, lax.axis_index("y"), lax.axis_index("zh"), odd_x]).astype(jnp.int32)
    cot = gather(out_grad, TP, 8)
    keys_in = swap(prefix_keys)
    values_in = swap(prefix_values)
    cot, keys_in, values_in = lax.optimization_barrier((cot, keys_in, values_in))
    tokens = (prefix_keys, keys_in, prefix_values, values_in)

    dout = dout_rows(place, cot, swap(cot), out_weight)
    dout = lax.all_to_all(dout, CHIPS, 0, 0, tiled=True)
    part, lse = forward(place, queries, *tokens)
    msg1, own_stats = message(part, lse, dout)
    msg1 = lax.all_to_all(msg1, CHIPS, 0, 0, tiled=True)
    cot_part = dout[:, NUM:]
    cot_other = lax.ppermute(cot_part, "x", [(0, 1), (1, 0), (2, 3), (3, 2)])
    sums, probs = query_parts(place, queries, dout, own_stats, *tokens)
    cot_mine = in_order(odd_x, cot_part, after(cot_other, sums), 1)
    cot_in = swap(cot_mine)

    msg1, cot_mine, cot_in = lax.optimization_barrier((msg1, cot_mine, cot_in))
    att64, stats, msg2 = combine(place, msg1, own_stats, sums)
    msg2 = lax.all_to_all(msg2, CHIPS, 0, 0, tiled=True)

    att32 = in_order(core, half(att64, core, 0), swap(half(att64, 1 - core, 0)), 1)
    partial_out = dot(att32, out_weight, 1, 0).reshape(32, 4, 1024).transpose(1, 0, 2)
    by_x = [
        lax.dynamic_index_in_dim(partial_out, lax.rem(at_x + d, 4), 0, keepdims=False)
        for d in range(4)
    ]
    from_x = [shift(by_x[d].astype(BF16), "x", d) for d in (1, 2, 3)]
    dk, dk_out, dv, dv_out = token_grads(
        place, queries, dout, own_stats, after(stats, by_x[0]), probs, prefix_values, values_in
    )
    own_x, *from_x = lax.optimization_barrier((by_x[0], *from_x, dk))[:4]
    over_x = own_x + sum(x.astype(F32) for x in from_x)
    by_zl = over_x.reshape(32, 2, 512).transpose(1, 0, 2)
    from_zl = lax.ppermute(
        lax.dynamic_index_in_dim(by_zl, 1 - at_zl, 0, keepdims=False).astype(BF16),
        "zl",
        [(0, 1), (1, 0)],
    )
    own_zl = lax.dynamic_index_in_dim(by_zl, at_zl, 0, keepdims=False)
    other_cols = (jnp.int32(0), ((1 - core) * WIDE).astype(jnp.int32))
    key_grad = lax.dynamic_update_slice(dk, swap(dk_out), other_cols)
    value_grad = lax.dynamic_update_slice(dv, swap(dv_out), other_cols)

    msg2, from_zl = lax.optimization_barrier((msg2, from_zl, key_grad, value_grad))[:2]
    latent_out = (own_zl + from_zl.astype(F32)).astype(BF16)
    dq64 = jnp.sum(msg2[:, :NUM].astype(F32), axis=0).astype(BF16)
    dq_in = swap(half(dq64, 1 - core, 0))
    query_grad = in_order(core, half(dq64, core, 0), dq_in, 1)
    weight_part = weight(place, msg2, cot_mine, cot_in)
    weight_in = swap(half(weight_part, 1 - core, 1))
    weight_grad = in_order(core, half(weight_part, core, 1), weight_in, 0)
    return latent_out, query_grad, key_grad, value_grad, weight_grad


def solution(mesh):
    fine = Mesh(mesh.devices.reshape(4, 4, 2, 4, 2), ("y", "zh", "core", "x", "zl"))
    placed = (P(None, TP), P(CTX, TP), P(CTX, TP), P(TP, None), P(CTX, TP))
    return jax.shard_map(
        body,
        mesh=fine,
        in_specs=placed,
        out_specs=(P(CTX, TP), P(CTX, TP), P(CTX, TP), P(CTX, TP), P(TP, CTX)),
        check_vma=False,
    )
```

```python
import math

import jax
import jax.numpy as jnp
from jax import lax
from jax.experimental import pallas as pl
from jax.experimental.pallas import tpu as pltpu
from jax.sharding import Mesh
from jax.sharding import PartitionSpec as P

HDIM = 128
SCALE = HDIM ** (-0.5)
LOG2E = math.log2(math.e)
EXP2_SCALE = SCALE * LOG2E
CHIPS = ("y", "zh")
CTX = ("y", "zh", "core")
TP = ("x", "zl")
N_CHIPS = 16
HEADS_HERE = 2
WIDE = HEADS_HERE * HDIM
NUM, STAT, COT, PART = 64, 48, 32, 16
ROWS1 = NUM + STAT
ROWS2 = NUM + NUM
ROWS0 = NUM + PART
LATENTS = N_CHIPS * NUM
F32 = jnp.float32
BF16 = jnp.bfloat16


def dot(a, b, ca, cb):
    return lax.dot_general(a, b, (((ca,), (cb,)), ((), ())), preferred_element_type=F32)


def in_three(x):
    high = x.astype(BF16)
    rest = x - high.astype(F32)
    middle = rest.astype(BF16)
    low = (rest - middle.astype(F32)).astype(BF16)
    return high, middle, low


def params(mib):
    return pltpu.CompilerParams(vmem_limit_bytes=mib * 1024 * 1024)


def whole(*shape):
    return pl.BlockSpec(shape, lambda *_: (0,) * len(shape))


def head_cols(h):
    return slice(h * HDIM, (h + 1) * HDIM)


def dout_kernel(place_ref, own_ref, other_ref, w_ref, out_ref, cot_ref):
    core = place_ref[0]
    for row, ref in ((core, own_ref), (1 - core, other_ref)):
        start = pl.multiple_of(row * COT, COT)
        for b in range(8):
            cot_ref[pl.ds(start, COT), b * 512 : (b + 1) * 512] = ref[b]
    dout = jnp.transpose(dot(w_ref[...], cot_ref[...], 1, 1)).astype(BF16)
    start = pl.multiple_of(core * COT + place_ref[3] * PART, PART)
    for c in range(N_CHIPS):
        out_ref[c, 0:NUM, :] = dout
        out_ref[c, NUM:, :] = cot_ref[pl.ds(start, PART), c * WIDE : (c + 1) * WIDE]


def dout_rows(place, cot, cot_in, out_weight):
    depth = out_weight.shape[1]
    grid_spec = pltpu.PrefetchScalarGridSpec(
        num_scalar_prefetch=1,
        grid=(1,),
        in_specs=[
            whole(8, COT, 512),
            whole(8, COT, 512),
            pl.BlockSpec((WIDE, depth), lambda i, c: (c[0], 0)),
        ],
        out_specs=whole(N_CHIPS, ROWS0, WIDE),
        scratch_shapes=[pltpu.VMEM((NUM, depth), BF16)],
    )
    return pl.pallas_call(
        dout_kernel,
        out_shape=jax.ShapeDtypeStruct((N_CHIPS, ROWS0, WIDE), BF16),
        grid_spec=grid_spec,
        compiler_params=params(60),
        name="dout",
    )(place, cot, cot_in, out_weight)


def forward_kernel(place_ref, q_ref, ko_ref, kr_ref, vo_ref, vr_ref, part_ref, lse_ref):
    heads = range(HEADS_HERE)
    scores = [
        [dot(k[:, head_cols(h)], q_ref[:, head_cols(h)], 1, 1) for k in (ko_ref, kr_ref)]
        for h in heads
    ]
    expos = []
    for h in heads:
        top = jnp.maximum(
            jnp.max(scores[h][0], axis=0, keepdims=True),
            jnp.max(scores[h][1], axis=0, keepdims=True),
        )
        shift = top * EXP2_SCALE
        expo = [jnp.exp2(s * EXP2_SCALE - shift) for s in scores[h]]
        den = jnp.sum(expo[0], axis=0, keepdims=True) + jnp.sum(expo[1], axis=0, keepdims=True)
        expos.append(([e.astype(BF16) for e in expo], den))
        lse_ref[h : h + 1, :] = top * SCALE + jnp.log(den)
    for h in heads:
        (own, other), den = expos[h]
        num = dot(vo_ref[:, head_cols(h)], own, 0, 0) + dot(vr_ref[:, head_cols(h)], other, 0, 0)
        part_ref[:, head_cols(h)] = jnp.transpose(num / den).astype(BF16)


def forward(place, queries, keys, keys_in, values, values_in):
    tokens = keys.shape[0]
    block = 512
    own = pl.BlockSpec((tokens, WIDE), lambda i, c: (0, c[0]))
    grid_spec = pltpu.PrefetchScalarGridSpec(
        num_scalar_prefetch=1,
        grid=(LATENTS // block,),
        in_specs=[
            pl.BlockSpec((block, WIDE), lambda i, c: (i, c[0])),
            own, own, own, own,
        ],
        out_specs=[
            pl.BlockSpec((block, WIDE), lambda i, c: (i, 0)),
            pl.BlockSpec((8, block), lambda i, c: (0, i)),
        ],
    )
    return pl.pallas_call(
        forward_kernel,
        out_shape=[
            jax.ShapeDtypeStruct((LATENTS, WIDE), BF16),
            jax.ShapeDtypeStruct((8, LATENTS), F32),
        ],
        grid_spec=grid_spec,
        compiler_params=params(60),
        cost_estimate=pl.CostEstimate(
            flops=9_000_000_000, bytes_accessed=4_000_000, transcendentals=4_194_304
        ),
        name="forward",
    )(place, queries, keys, keys_in, values, values_in)


def message_kernel(part_ref, lse_ref, dout_ref, msg_ref, stat_ref):
    rows = []
    deltas = []
    stat_ref[...] = jnp.zeros_like(stat_ref)
    for h in range(HEADS_HERE):
        cols = head_cols(h)
        dout = dout_ref[:, :, cols].reshape(LATENTS, HDIM).astype(F32)
        delta = jnp.sum(part_ref[:, cols].astype(F32) * dout, axis=1, keepdims=True)
        deltas.append(jnp.transpose(jnp.broadcast_to(delta, (LATENTS, HDIM)))[0:1, :])
        stat_ref[h : h + 1, :] = lse_ref[h : h + 1, :] * LOG2E
        stat_ref[2 + h : 3 + h, :] = deltas[h]
    for h in range(HEADS_HERE):
        rows.extend(in_three(lse_ref[h : h + 1, :]))
    for h in range(HEADS_HERE):
        rows.extend(in_three(deltas[h]))
    stats = jnp.concatenate(rows, axis=0)
    stats = jnp.concatenate([stats[:, i * WIDE : (i + 1) * WIDE] for i in range(4)], axis=0)
    for c in range(N_CHIPS):
        msg_ref[c, 0:NUM, :] = part_ref[c * NUM : (c + 1) * NUM, :]
        msg_ref[c, NUM:, :] = stats


def message(part, lse, dout):
    return pl.pallas_call(
        message_kernel,
        out_shape=[
            jax.ShapeDtypeStruct((N_CHIPS, ROWS1, WIDE), BF16),
            jax.ShapeDtypeStruct((8, LATENTS), F32),
        ],
        grid=(1,),
        in_specs=[whole(LATENTS, WIDE), whole(8, LATENTS), whole(N_CHIPS, NUM, WIDE)],
        out_specs=[whole(N_CHIPS, ROWS1, WIDE), whole(8, LATENTS)],
        compiler_params=params(60),
        name="message",
    )(part, lse, dout)


def combine_kernel(
    place_ref, msg_ref, own_ref, sums_ref, att_ref, stat_ref, out_ref
):
    y = place_ref[1]
    zh = place_ref[2]
    mine = [jnp.zeros((N_CHIPS, WIDE), F32) for _ in range(HEADS_HERE)]
    stat_ref[...] = jnp.zeros_like(stat_ref)
    for i in range(4):
        blocks = [msg_ref[c, NUM:, :].astype(F32) for c in range(N_CHIPS)]
        cols = slice(i * WIDE, (i + 1) * WIDE)

        def value(r):
            at = 12 * i + 3 * r
            return jnp.concatenate(
                [b[at : at + 1] + b[at + 1 : at + 2] + b[at + 2 : at + 3] for b in blocks], axis=0
            )

        for h in range(HEADS_HERE):
            lse = value(h)
            delta = value(2 + h)
            top = jnp.max(lse, axis=0, keepdims=True)
            total = top + jnp.log(jnp.sum(jnp.exp(lse - top), axis=0, keepdims=True))
            weight = jnp.exp(lse - total)
            stat_ref[h : h + 1, cols] = total * LOG2E
            stat_ref[2 + h : 3 + h, cols] = jnp.sum(weight * delta, axis=0, keepdims=True)
            mine[h] = jnp.where(y == i, weight, mine[h])
    att_all = []
    for h in range(HEADS_HERE):
        rows = jnp.zeros((N_CHIPS, NUM), F32)
        for z in range(4):
            rows = jnp.where(zh == z, mine[h][:, z * NUM : (z + 1) * NUM], rows)
        weight = jnp.transpose(rows)
        att = jnp.zeros((NUM, HDIM), F32)
        for c in range(N_CHIPS):
            att = att + msg_ref[c, 0:NUM, head_cols(h)].astype(F32) * weight[:, c : c + 1]
        att_all.append(att.astype(BF16))
    att = jnp.concatenate(att_all, axis=1)
    att_ref[...] = att
    for c in range(N_CHIPS):
        out_ref[c, NUM:, :] = att
    for h in range(HEADS_HERE):
        cols = head_cols(h)
        share = jnp.exp2(own_ref[h : h + 1, :] - stat_ref[h : h + 1, :]) * SCALE
        rest = stat_ref[2 + h : 3 + h, :] - own_ref[2 + h : 3 + h, :]
        at_scores = sums_ref[0, cols, :].astype(F32)
        at_probs = sums_ref[1, cols, :].astype(F32)
        dq = jnp.transpose(share * (at_scores - rest * at_probs)).astype(BF16)
        out_ref[:, 0:NUM, cols] = dq.reshape(N_CHIPS, NUM, HDIM)


def combine(place, msg, own_stats, sums):
    grid_spec = pltpu.PrefetchScalarGridSpec(
        num_scalar_prefetch=1,
        grid=(1,),
        in_specs=[
            whole(N_CHIPS, ROWS1, WIDE), whole(8, LATENTS),
            whole(2, WIDE, LATENTS),
        ],
        out_specs=[whole(NUM, WIDE), whole(8, LATENTS), whole(N_CHIPS, ROWS2, WIDE)],
    )
    return pl.pallas_call(
        combine_kernel,
        out_shape=[
            jax.ShapeDtypeStruct((NUM, WIDE), BF16),
            jax.ShapeDtypeStruct((8, LATENTS), F32),
            jax.ShapeDtypeStruct((N_CHIPS, ROWS2, WIDE), BF16),
        ],
        grid_spec=grid_spec,
        compiler_params=params(24),
        name="combine",
    )(place, msg, own_stats, sums)


def query_kernel(
    place_ref, q_ref, dout_ref, stat_ref, ko_ref, kr_ref, vo_ref, vr_ref,
    sums_ref, prob_ref,
):
    h = pl.program_id(0)
    block = 256
    for at in range(0, LATENTS, block):
        rows = slice(at, at + block)
        q = q_ref[rows, :]
        dout = dout_ref[at // NUM : (at + block) // NUM].reshape(block, HDIM)
        lse = stat_ref[pl.ds(h, 1), rows]
        delta = stat_ref[pl.ds(2 + h, 1), rows]
        a = 0
        b = 0
        for src, (k_ref, v_ref) in enumerate(((ko_ref, vo_ref), (kr_ref, vr_ref))):
            k = k_ref[...]
            probs = jnp.exp2(dot(k, q, 1, 1) * EXP2_SCALE - lse)
            dscore = (probs * (dot(v_ref[...], dout, 1, 1) - delta)).astype(BF16)
            probs = probs.astype(BF16)
            prob_ref[0, src, :, rows] = probs
            a = a + dot(k, dscore, 0, 0)
            b = b + dot(k, probs, 0, 0)
        sums_ref[0, :, rows] = a.astype(BF16)
        sums_ref[1, :, rows] = b.astype(BF16)


def query_parts(place, queries, dout, stats, keys, keys_in, values, values_in):
    tokens = keys.shape[0]
    head = pl.BlockSpec((tokens, HDIM), lambda h, c: (0, c[0] * HEADS_HERE + h))
    sums = pl.BlockSpec((2, HDIM, LATENTS), lambda h, c: (0, h, 0))
    kept = pl.BlockSpec((1, 2, tokens, LATENTS), lambda h, c: (h, 0, 0, 0))
    grid_spec = pltpu.PrefetchScalarGridSpec(
        num_scalar_prefetch=1,
        grid=(HEADS_HERE,),
        in_specs=[
            pl.BlockSpec((LATENTS, HDIM), lambda h, c: (0, c[0] * HEADS_HERE + h)),
            pl.BlockSpec((N_CHIPS, NUM, HDIM), lambda h, c: (0, 0, h)),
            whole(8, LATENTS),
            head, head, head, head,
        ],
        out_specs=[sums, kept],
    )
    return pl.pallas_call(
        query_kernel,
        out_shape=[
            jax.ShapeDtypeStruct((2, WIDE, LATENTS), BF16),
            jax.ShapeDtypeStruct((HEADS_HERE, 2, tokens, LATENTS), BF16),
        ],
        grid_spec=grid_spec,
        compiler_params=params(60),
        cost_estimate=pl.CostEstimate(
            flops=12_000_000_000, bytes_accessed=20_000_000, transcendentals=4_194_304
        ),
        name="query",
    )(place, queries, dout, stats, keys, keys_in, values, values_in)


def token_kernel(
    place_ref, q_ref, dout_ref, own_ref, stat_ref, prob_ref, vo_ref, vr_ref,
    dko_ref, dkr_ref, dvo_ref, dvr_ref, dout_scaled_ref, q_scaled_ref,
):
    h = pl.program_id(0)

    @pl.when(pl.program_id(1) == 0)
    def _():
        share = jnp.exp2(own_ref[pl.ds(h, 1), :] - stat_ref[pl.ds(h, 1), :])
        share = jnp.transpose(jnp.broadcast_to(share, (HDIM, LATENTS)))
        dout = dout_ref[...].reshape(LATENTS, HDIM).astype(F32)
        dout_scaled_ref[...] = (share * dout).astype(BF16)
        q_scaled_ref[...] = (share * q_ref[...].astype(F32)).astype(BF16)

    delta = stat_ref[pl.ds(2 + h, 1), :]
    dout = dout_ref[...].reshape(LATENTS, HDIM)
    dprobs = [dot(v_ref[...], dout, 1, 1) for v_ref in (vo_ref, vr_ref)]
    dv = [dot(prob_ref[0, src], dout_scaled_ref[...], 1, 0) for src in (0, 1)]
    dscores = [
        (prob_ref[0, src].astype(F32) * (dprobs[src] - delta)).astype(BF16) for src in (0, 1)
    ]
    dk = [dot(dscores[src], q_scaled_ref[...], 1, 0) for src in (0, 1)]
    for src, (dk_ref, dv_ref) in enumerate(((dko_ref, dvo_ref), (dkr_ref, dvr_ref))):
        dv_ref[...] = dv[src].astype(BF16)
        dk_ref[...] = (dk[src] * SCALE).astype(BF16)


def token_grads(place, queries, dout, own_stats, stats, probs, values, values_in):
    tokens = probs.shape[2]
    block = 512
    own = pl.BlockSpec((block, HDIM), lambda h, i, c: (i, c[0] * HEADS_HERE + h))
    other = pl.BlockSpec((block, HDIM), lambda h, i, c: (i, h))
    kept = pl.BlockSpec((1, 2, block, LATENTS), lambda h, i, c: (h, 0, i, 0))
    grid_spec = pltpu.PrefetchScalarGridSpec(
        num_scalar_prefetch=1,
        grid=(HEADS_HERE, tokens // block),
        in_specs=[
            pl.BlockSpec((LATENTS, HDIM), lambda h, i, c: (0, c[0] * HEADS_HERE + h)),
            pl.BlockSpec((N_CHIPS, NUM, HDIM), lambda h, i, c: (0, 0, h)),
            whole(8, LATENTS),
            whole(8, LATENTS),
            kept, own, own,
        ],
        out_specs=[own, other, own, other],
        scratch_shapes=[pltpu.VMEM((LATENTS, HDIM), BF16), pltpu.VMEM((LATENTS, HDIM), BF16)],
    )
    full = jax.ShapeDtypeStruct((tokens, 2 * WIDE), BF16)
    half_wide = jax.ShapeDtypeStruct((tokens, WIDE), BF16)
    return pl.pallas_call(
        token_kernel,
        out_shape=[full, half_wide, full, half_wide],
        grid_spec=grid_spec,
        compiler_params=params(60),
        cost_estimate=pl.CostEstimate(
            flops=8_000_000_000, bytes_accessed=14_000_000, transcendentals=0
        ),
        name="token",
    )(place, queries, dout, own_stats, stats, probs, values, values_in)


def weight_kernel(place_ref, att_ref, own_ref, other_ref, out_ref, cot_ref):
    core = place_ref[0]
    cot_ref[:, pl.ds(pl.multiple_of(core * COT, COT), COT), :] = own_ref[...]
    cot_ref[:, pl.ds(pl.multiple_of((1 - core) * COT, COT), COT), :] = other_ref[...]
    att = att_ref[...].reshape(LATENTS, WIDE)
    cot = cot_ref[...].reshape(LATENTS, WIDE)
    out_ref[...] = dot(att, cot, 0, 0)


def weight(place, msg, cot, cot_in):
    grid_spec = pltpu.PrefetchScalarGridSpec(
        num_scalar_prefetch=1,
        grid=(1,),
        in_specs=[
            pl.BlockSpec((N_CHIPS, NUM, WIDE), lambda i, c: (0, 1, 0)),
            whole(N_CHIPS, COT, WIDE),
            whole(N_CHIPS, COT, WIDE),
        ],
        out_specs=whole(WIDE, WIDE),
        scratch_shapes=[pltpu.VMEM((N_CHIPS, NUM, WIDE), BF16)],
    )
    return pl.pallas_call(
        weight_kernel,
        out_shape=jax.ShapeDtypeStruct((WIDE, WIDE), F32),
        grid_spec=grid_spec,
        compiler_params=params(24),
        name="weight",
    )(place, msg, cot, cot_in)


def swap(x):
    return lax.ppermute(x, "core", [(0, 1), (1, 0)])


def half(x, index, axis):
    size = x.shape[axis] // 2
    return lax.dynamic_slice_in_dim(x, index * size, size, axis)


def in_order(core, mine, other, axis):
    return jnp.where(
        core == 0,
        jnp.concatenate([mine, other], axis),
        jnp.concatenate([other, mine], axis),
    )


def gather(x, axes, size):
    tiled = jnp.broadcast_to(x[None], (size,) + x.shape)
    return lax.all_to_all(tiled, axes, 0, 0, tiled=True)


def shift(x, axis, d):
    return lax.ppermute(x, axis, [(i, (i + d) % 4) for i in range(4)])


def after(x, *others):
    return lax.optimization_barrier((x,) + others)[0]


def body(queries, prefix_keys, prefix_values, out_weight, out_grad):
    core = lax.axis_index("core")
    at_x, at_zl = lax.axis_index("x"), lax.axis_index("zl")
    odd_x = lax.rem(at_x, 2)
    place = jnp.stack([core, lax.axis_index("y"), lax.axis_index("zh"), odd_x]).astype(jnp.int32)
    cot = gather(out_grad, TP, 8)
    keys_in = swap(prefix_keys)
    values_in = swap(prefix_values)
    cot, keys_in, values_in = lax.optimization_barrier((cot, keys_in, values_in))
    tokens = (prefix_keys, keys_in, prefix_values, values_in)

    dout = dout_rows(place, cot, swap(cot), out_weight)
    dout = lax.all_to_all(dout, CHIPS, 0, 0, tiled=True)
    part, lse = forward(place, queries, *tokens)
    msg1, own_stats = message(part, lse, dout)
    msg1 = lax.all_to_all(msg1, CHIPS, 0, 0, tiled=True)
    cot_part = dout[:, NUM:]
    cot_other = lax.ppermute(cot_part, "x", [(0, 1), (1, 0), (2, 3), (3, 2)])
    sums, probs = query_parts(place, queries, dout, own_stats, *tokens)
    cot_mine = in_order(odd_x, cot_part, after(cot_other, sums), 1)
    cot_in = swap(cot_mine)

    msg1, cot_mine, cot_in = lax.optimization_barrier((msg1, cot_mine, cot_in))
    att64, stats, msg2 = combine(place, msg1, own_stats, sums)
    msg2 = lax.all_to_all(msg2, CHIPS, 0, 0, tiled=True)

    att32 = in_order(core, half(att64, core, 0), swap(half(att64, 1 - core, 0)), 1)
    partial_out = dot(att32, out_weight, 1, 0).reshape(32, 4, 1024).transpose(1, 0, 2)
    by_x = [
        lax.dynamic_index_in_dim(partial_out, lax.rem(at_x + d, 4), 0, keepdims=False)
        for d in range(4)
    ]
    from_x = [shift(by_x[d].astype(BF16), "x", d) for d in (1, 2, 3)]
    dk, dk_out, dv, dv_out = token_grads(
        place, queries, dout, own_stats, after(stats, by_x[0]), probs, prefix_values, values_in
    )
    own_x, *from_x = lax.optimization_barrier((by_x[0], *from_x, dk))[:4]
    over_x = own_x + sum(x.astype(F32) for x in from_x)
    by_zl = over_x.reshape(32, 2, 512).transpose(1, 0, 2)
    from_zl = lax.ppermute(
        lax.dynamic_index_in_dim(by_zl, 1 - at_zl, 0, keepdims=False).astype(BF16),
        "zl",
        [(0, 1), (1, 0)],
    )
    own_zl = lax.dynamic_index_in_dim(by_zl, at_zl, 0, keepdims=False)
    other_cols = (jnp.int32(0), ((1 - core) * WIDE).astype(jnp.int32))
    key_grad = lax.dynamic_update_slice(dk, swap(dk_out), other_cols)
    value_grad = lax.dynamic_update_slice(dv, swap(dv_out), other_cols)

    from_zl = after(from_zl, key_grad, value_grad)
    latent_out = (own_zl + from_zl.astype(F32)).astype(BF16)
    msg2 = after(msg2, latent_out)
    dq64 = jnp.sum(msg2[:, :NUM].astype(F32), axis=0).astype(BF16)
    dq_in = swap(half(dq64, 1 - core, 0))
    query_grad = in_order(core, half(dq64, core, 0), dq_in, 1)
    weight_part = weight(place, msg2, cot_mine, cot_in)
    weight_in = swap(half(weight_part, 1 - core, 1))
    weight_grad = in_order(core, half(weight_part, core, 1), weight_in, 0)
    return latent_out, query_grad, key_grad, value_grad, weight_grad


def solution(mesh):
    fine = Mesh(mesh.devices.reshape(4, 4, 2, 4, 2), ("y", "zh", "core", "x", "zl"))
    placed = (P(None, TP), P(CTX, TP), P(CTX, TP), P(TP, None), P(CTX, TP))
    return jax.shard_map(
        body,
        mesh=fine,
        in_specs=placed,
        out_specs=(P(CTX, TP), P(CTX, TP), P(CTX, TP), P(CTX, TP), P(TP, CTX)),
        check_vma=False,
    )
```
